256 devices in a mesh: ta: 2 (over x_lo), ha: 4 (over x_hi, core), wa: 32 (over z, y).
Axes of the slice: x: 4 (x_hi: 2, x_lo: 2; x = x_hi * 2 + x_lo), y: 4, z: 8, core: 2. Of those that a mesh axis runs over, the one named last changes fastest.
Arguments:
- queries: bfloat16 [32, 2, 4, 192, 1536], P('wa', 'ta', 'ha'), may hold values from -5 to 5
- keys_values: bfloat16 [2, 32, 2, 4, 192, 1536], P(None, 'wa', 'ta', 'ha'), may hold values from -5 to 5
- upstream: bfloat16 [32, 2, 4, 192, 1536], P('wa', 'ta', 'ha'), may hold values from -1.5 to 1.5
- out_weight: bfloat16 [32, 1536, 1536], P(None, 'wa'), may hold values from -1.25 to 1.25
- block_pick: int32 [1], replicated, may hold values from 0 to 31
Outputs:
- mixed: bfloat16 [32, 2, 4, 192, 1536], P('wa', 'ta', 'ha')
- grad_queries: bfloat16 [32, 2, 4, 192, 1536], P('wa', 'ta', 'ha')
- grad_keys_values: bfloat16 [2, 32, 2, 4, 192, 1536], P(None, 'wa', 'ta', 'ha')
- grad_weight: float32 [1536, 1536], P('wa')
The draws below stay inside these ranges and needn't reach their ends.
All inputs are finite; a program needn't handle non-finite values.
Results may differ from the reference program's by a relative error of at most 0.029.
Values may be sent and summed in bfloat16 or wider, within the bound.
No kernel may reach another device: no remote copies, remote signals or barrier semaphores. Data moves between devices by JAX's collectives and lax.ppermute only.
A program may use at most 128 MiB of HBM per device.

```python
import jax
import jax.numpy as jnp
from jax import lax

HEADS = 12
HEAD_DIM = 128
HD = 1536
DOUT = 1536
TILE = 192
TT = 2
HT = 4
SAMPLES = 32
CAND = 32


def draw_queries(key, part):
    key = jax.random.fold_in(key, 31)
    shape = (SAMPLES, TT, HT, TILE, HD)
    base = jax.random.truncated_normal(key, -4.0, 4.0, shape, jnp.float32)
    return base.astype(jnp.bfloat16)


def draw_keys_values(key, part):
    key = jax.random.fold_in(key, 47)
    shape = (2, SAMPLES, TT, HT, TILE, HD)
    base = jax.random.truncated_normal(key, -4.0, 4.0, shape, jnp.float32)
    return base.astype(jnp.bfloat16)


def shard_levels(own_key, extent, cuts, low, largest):
    gain = 1.0
    for axis_at, blocks in cuts:
        draws = jax.random.uniform(jax.random.fold_in(jax.random.fold_in(own_key, 6), axis_at), (blocks,), jnp.float32, low / len(cuts), largest / len(cuts))
        gain = gain * jnp.repeat(jnp.exp(draws), extent[axis_at] // blocks).reshape((-1,) + (1,) * (len(extent) - 1 - axis_at))
    return gain


def noise(key, shape, spread, bound, shards=(), kind=jnp.bfloat16):
    loudness = shard_levels(key, shape, shards, -0.22, 0.18) if shards else 1.0
    array = jax.random.normal(key, shape, jnp.float32) * spread * loudness
    return jnp.minimum(jnp.maximum(array, -bound), bound).astype(kind)


def setup_inputs(seed: int = 0) -> dict:
    arg_keys = jax.random.split(jax.random.key(seed), 6)
    return {
        "queries": draw_queries(jax.random.fold_in(arg_keys[5], 71), 0),
        "keys_values": draw_keys_values(jax.random.fold_in(arg_keys[5], 71), 0),
        "upstream": noise(arg_keys[2], (SAMPLES, TT, HT, TILE, DOUT), 0.25, 1.5, ((0, 32), (1, 2), (2, 4))),
        "out_weight": noise(arg_keys[3], (CAND, HD, DOUT), (max(HD // 64, 1)) ** -0.5, 1.25, ((1, 32),)),
        "block_pick": jax.random.randint(arg_keys[4], (1,), 0, CAND).astype(jnp.int32),
    }


def split_heads(block):
    return block.reshape(block.shape[:-1] + (HEADS, HEAD_DIM))


def live_slots():
    time_tile = jnp.arange(TT, dtype=jnp.int32)[:, None]
    height_tile = jnp.arange(HT, dtype=jnp.int32)[None, :]
    own = jnp.ones((TT, HT), dtype=bool)
    earlier = jnp.broadcast_to(time_tile > 0, (TT, HT))
    later = jnp.broadcast_to(time_tile < TT - 1, (TT, HT))
    upper = jnp.broadcast_to(height_tile > 0, (TT, HT))
    lower = jnp.broadcast_to(height_tile < HT - 1, (TT, HT))
    slots = jnp.stack([own, earlier, later, upper, lower], axis=-1)
    return jnp.repeat(slots, TILE, axis=-1)


def windows(pair_s):
    padded = jnp.pad(pair_s, ((0, 0), (1, 1), (1, 1), (0, 0), (0, 0)))
    parts = [padded[:, 1:-1, 1:-1], padded[:, :-2, 1:-1], padded[:, 2:, 1:-1], padded[:, 1:-1, :-2], padded[:, 1:-1, 2:]]
    return jnp.concatenate(parts, axis=3)


def attend_forward(queries, keys, values, live):
    scale = HEAD_DIM ** -0.5
    scores = jnp.einsum("...qhd,...khd->...hqk", queries.astype(jnp.float32), keys.astype(jnp.float32)) * scale
    scores = jnp.where(live[:, :, None, None, :], scores, -jnp.inf)
    top = jnp.max(scores, axis=-1, keepdims=True)
    weights = jnp.exp(scores - top)
    probs = weights / jnp.sum(weights, axis=-1, keepdims=True)
    probs_b = probs.astype(jnp.bfloat16)
    attention = jnp.einsum("...hqk,...khd->...qhd", probs_b.astype(jnp.float32), values.astype(jnp.float32))
    return probs, probs_b, attention.astype(jnp.bfloat16)


def move_time(block, forward):
    zeros = jnp.zeros_like(block[:, :1])
    if forward:
        return jnp.concatenate([zeros, block[:, :-1]], axis=1)
    return jnp.concatenate([block[:, 1:], zeros], axis=1)


def move_height(block, forward):
    zeros = jnp.zeros_like(block[:, :, :1])
    if forward:
        return jnp.concatenate([zeros, block[:, :, :-1]], axis=2)
    return jnp.concatenate([block[:, :, 1:], zeros], axis=2)


def reference(queries, keys_values, upstream, out_weight, block_pick):
    live = live_slots()
    weight = lax.dynamic_index_in_dim(out_weight, block_pick[0], 0, keepdims=False)
    per_sample = jnp.moveaxis(keys_values, 1, 0)

    def forward_one(pair):
        query_s, pair_s = pair
        window = windows(pair_s)
        _, _, attention = attend_forward(split_heads(query_s), split_heads(window[0]), split_heads(window[1]), live)
        return attention.reshape(query_s.shape)

    attention = lax.map(forward_one, (queries, per_sample))
    flat = attention.reshape(-1, HD)
    up_flat = upstream.reshape(-1, DOUT)
    mixed = jnp.dot(flat, weight, preferred_element_type=jnp.float32).astype(jnp.bfloat16).reshape(upstream.shape)
    d_attention = jnp.dot(up_flat, weight.T, preferred_element_type=jnp.float32).astype(jnp.bfloat16).reshape(attention.shape)
    grad_weight = jnp.dot(flat.T, up_flat, preferred_element_type=jnp.float32)
    scale = HEAD_DIM ** -0.5

    def backward_one(triple):
        query_s, pair_s, d_att_s = triple
        window = windows(pair_s)
        heads_q = split_heads(query_s)
        keys = split_heads(window[0])
        values = split_heads(window[1])
        probs, probs_b, attention_s = attend_forward(heads_q, keys, values, live)
        d_att = split_heads(d_att_s)
        delta = jnp.sum(d_att.astype(jnp.float32) * attention_s.astype(jnp.float32), axis=-1)
        delta = jnp.swapaxes(delta, -1, -2)[..., None]
        d_probs = jnp.einsum("...qhd,...khd->...hqk", d_att.astype(jnp.float32), values.astype(jnp.float32))
        d_scores = (probs * (d_probs - delta)).astype(jnp.bfloat16)
        grad_q = jnp.einsum("...hqk,...khd->...qhd", d_scores.astype(jnp.float32), keys.astype(jnp.float32)) * scale
        key_terms = jnp.einsum("...hqk,...qhd->...khd", d_scores.astype(jnp.float32), heads_q.astype(jnp.float32)) * scale
        value_terms = jnp.einsum("...hqk,...qhd->...khd", probs_b.astype(jnp.float32), d_att.astype(jnp.float32))
        terms = jnp.stack([key_terms, value_terms]).reshape((2, TT, HT, 5 * TILE, HD))
        total = terms[:, :, :, :TILE]
        sent = terms[:, :, :, TILE:].astype(jnp.bfloat16).astype(jnp.float32)
        total = total + move_time(sent[:, :, :, 0:TILE], False)
        total = total + move_time(sent[:, :, :, TILE:2 * TILE], True)
        total = total + move_height(sent[:, :, :, 2 * TILE:3 * TILE], False)
        total = total + move_height(sent[:, :, :, 3 * TILE:], True)
        return grad_q.astype(jnp.bfloat16).reshape(query_s.shape), total.astype(jnp.bfloat16)

    grad_queries, grad_pairs = lax.map(backward_one, (queries, per_sample, d_attention))
    grad_keys_values = jnp.moveaxis(grad_pairs, 0, 1)
    return mixed, grad_queries, grad_keys_values, grad_weight
```

```python
import functools

import jax
import jax.numpy as jnp
from jax import lax
from jax.experimental import pallas as pl
from jax.experimental.pallas import tpu as pltpu
from jax.sharding import Mesh, PartitionSpec as P

HEADS = 12
HEAD_DIM = 128
SCALE = HEAD_DIM ** (-0.5)
TILE = 192
SLOTS = 4
PER_STEP = 2
NT = (((1,), (1,)), ((), ()))
TN = (((0,), (0,)), ((), ()))
F32 = jnp.float32
BF16 = jnp.bfloat16


def window_of(refs, which, cols):
    return jnp.concatenate([ref[which, :, cols] for ref in refs], axis=0)


def probs_of(q, k, bound):
    scores = lax.dot_general(q, k, NT, preferred_element_type=F32)
    column = lax.broadcasted_iota(jnp.int32, scores.shape, 1)
    scores = jnp.where(column < bound, scores, -1e30)
    top = jnp.max(scores, axis=1, keepdims=True)
    weights = jnp.exp((scores - top) * SCALE)
    return weights * (1.0 / jnp.sum(weights, axis=1, keepdims=True))


def forward_kernel(bound_ref, q_ref, own_ref, time_ref, core_ref, cross_ref, out_ref):
    kv = (own_ref, time_ref, core_ref, cross_ref)
    for h in range(PER_STEP):
        cols = slice(h * HEAD_DIM, (h + 1) * HEAD_DIM)
        k = window_of(kv, 0, cols)
        v = window_of(kv, 1, cols)
        probs = probs_of(q_ref[:, cols], k, bound_ref[0])
        out = jnp.dot(probs.astype(BF16), v, preferred_element_type=F32)
        out_ref[:, cols] = out.astype(BF16)


def backward_kernel(
    bound_ref, q_ref, own_ref, time_ref, core_ref, cross_ref, att_ref, d_ref,
    gq_ref, g_own_ref, g_time_ref, g_core_ref, g_cross_ref,
):
    kv = (own_ref, time_ref, core_ref, cross_ref)
    outs = (g_own_ref, g_time_ref, g_core_ref, g_cross_ref)
    for h in range(PER_STEP):
        cols = slice(h * HEAD_DIM, (h + 1) * HEAD_DIM)
        q = q_ref[:, cols]
        k = window_of(kv, 0, cols)
        v = window_of(kv, 1, cols)
        d = d_ref[:, cols]
        probs = probs_of(q, k, bound_ref[0])
        delta = jnp.sum(d.astype(F32) * att_ref[:, cols].astype(F32), axis=1, keepdims=True)
        d_probs = lax.dot_general(d, v, NT, preferred_element_type=F32)
        d_scores = (probs * (d_probs - delta)).astype(BF16)
        value_terms = lax.dot_general(probs.astype(BF16), d, TN, preferred_element_type=F32)
        key_terms = lax.dot_general(d_scores, q, TN, preferred_element_type=F32) * SCALE
        gq = jnp.dot(d_scores, k, preferred_element_type=F32) * SCALE
        gq_ref[:, cols] = gq.astype(BF16)
        for s, ref in enumerate(outs):
            rows = slice(s * TILE, (s + 1) * TILE)
            ref[0, :, cols] = key_terms[rows].astype(ref.dtype)
            ref[1, :, cols] = value_terms[rows].astype(ref.dtype)


def flat_spec(first):
    return pl.BlockSpec((TILE, PER_STEP * HEAD_DIM), lambda i, b: (0, i + first))


def pair_spec(first):
    return pl.BlockSpec((2, TILE, PER_STEP * HEAD_DIM), lambda i, b: (0, 0, i + first))


def attention_forward(bound, q, kvs, heads):
    steps = heads // PER_STEP
    width = heads * HEAD_DIM
    return pl.pallas_call(
        forward_kernel,
        grid_spec=pltpu.PrefetchScalarGridSpec(
            num_scalar_prefetch=1,
            grid=(steps,),
            in_specs=[flat_spec(0)] + [pair_spec(0)] * 4,
            out_specs=flat_spec(0),
        ),
        out_shape=jax.ShapeDtypeStruct((TILE, width), BF16),
        compiler_params=pltpu.CompilerParams(vmem_limit_bytes=32 * 1024 * 1024),
        cost_estimate=pl.CostEstimate(
            flops=4 * heads * TILE * SLOTS * TILE * HEAD_DIM,
            bytes_accessed=2 * TILE * width * 10,
            transcendentals=heads * TILE * SLOTS * TILE,
        ),
    )(bound, q, *kvs)


def attention_backward(bound, q, kvs, att, d, first, heads):
    steps = heads // PER_STEP
    width = heads * HEAD_DIM
    at = first // PER_STEP
    return pl.pallas_call(
        backward_kernel,
        grid_spec=pltpu.PrefetchScalarGridSpec(
            num_scalar_prefetch=1,
            grid=(steps,),
            in_specs=[flat_spec(at)] + [pair_spec(at)] * 4 + [flat_spec(at)] * 2,
            out_specs=[flat_spec(0)] + [pair_spec(0)] * 4,
        ),
        out_shape=[jax.ShapeDtypeStruct((TILE, width), BF16), jax.ShapeDtypeStruct((2, TILE, width), F32)]
        + [jax.ShapeDtypeStruct((2, TILE, width), BF16)] * 3,
        compiler_params=pltpu.CompilerParams(vmem_limit_bytes=32 * 1024 * 1024),
        cost_estimate=pl.CostEstimate(
            flops=12 * heads * TILE * SLOTS * TILE * HEAD_DIM,
            bytes_accessed=2 * TILE * width * 24,
            transcendentals=heads * TILE * SLOTS * TILE,
        ),
    )(bound, q, *kvs, att, d)


SWAP = [(0, 1), (1, 0)]
CROSS = [(1, 2), (2, 1)]


def exchange(time, core, cross):
    return (
        lax.ppermute(time, "xl", SWAP),
        lax.ppermute(core, "co", SWAP),
        lax.ppermute(cross, ("xh", "co"), CROSS),
    )


def per_device(queries, keys_values, upstream, out_weight, block_pick):
    width = queries.shape[4]
    dout = upstream.shape[4]
    half = dout // 2
    ny = lax.axis_size("y")
    nz = lax.axis_size("z")
    xh = lax.axis_index("xh")
    co = lax.axis_index("co")
    y = lax.axis_index("y")
    q = queries.reshape(TILE, width)
    kv = keys_values.reshape(2, TILE, width)
    up = upstream.reshape(TILE, dout)

    has_cross = xh != co
    bound = jnp.where(has_cross, SLOTS * TILE, (SLOTS - 1) * TILE).astype(jnp.int32).reshape(1)

    panel = lax.dynamic_slice(out_weight, (block_pick[0], 0, co * half), (1, out_weight.shape[1], half))[0]
    w_mine = lax.all_gather(panel, ("z", "y"), axis=0, tiled=True)
    kvs = (kv,) + exchange(kv, kv, kv)
    w_mate = lax.ppermute(w_mine, "co", SWAP)

    up_mine = lax.dynamic_slice_in_dim(up, co * half, half, axis=1)
    up_mate = lax.dynamic_slice_in_dim(up, (1 - co) * half, half, axis=1)
    up_from_mate = lax.ppermute(up_mate, "co", SWAP)

    att = attention_forward(bound, q, kvs, HEADS)
    att_mate = lax.ppermute(att, "co", SWAP)

    d_att = (
        lax.dot_general(up_mine, w_mine, NT, preferred_element_type=F32)
        + lax.dot_general(up_mate, w_mate, NT, preferred_element_type=F32)
    ).astype(BF16)

    grad = lax.dot_general(att, up_mine, TN, preferred_element_type=F32) + lax.dot_general(
        att_mate, up_from_mate, TN, preferred_element_type=F32
    )
    rows = out_weight.shape[1]
    grad = grad.reshape(nz, ny, rows, half)
    total_w = lax.dynamic_index_in_dim(grad, y, 1, keepdims=False)
    grad_b = grad.astype(BF16)
    for k in range(1, ny):
        piece = lax.dynamic_index_in_dim(grad_b, lax.rem(y + k, ny), 1, keepdims=False)
        got = lax.ppermute(piece, "y", [(i, (i + k) % ny) for i in range(ny)])
        total_w = total_w + got.astype(F32)
    over_z = lax.all_to_all(total_w.astype(BF16), "z", split_axis=0, concat_axis=0, tiled=True)
    over_z = jnp.sum(over_z.astype(F32), axis=0).astype(BF16)
    x_near = lax.ppermute(over_z, "xl", SWAP)
    x_far = lax.ppermute(over_z, "xh", SWAP)
    x_both = lax.ppermute(over_z, ("xl", "xh"), [(i, 3 - i) for i in range(4)])
    mine = (over_z.astype(F32) + x_near.astype(F32)) + (x_far.astype(F32) + x_both.astype(F32))
    mate = lax.ppermute(mine, "co", SWAP)
    first = co == 0
    grad_weight = jnp.concatenate(
        [jnp.where(first, mine, mate), jnp.where(first, mate, mine)], axis=1
    )

    parts = 2
    heads = HEADS // parts
    gq_parts, gkv_parts = [], []
    for c in range(parts):
        gq, own, to_time, to_core, to_cross = attention_backward(
            bound, q, kvs, att, d_att, c * heads, heads
        )
        gq_parts.append(gq)
        from_time, from_core, from_cross = exchange(to_time, to_core, to_cross)
        gkv_parts.append(
            own + from_time.astype(F32) + from_core.astype(F32) + from_cross.astype(F32)
        )
    grad_q = jnp.concatenate(gq_parts, axis=1)
    grad_kv = jnp.concatenate([p.astype(BF16) for p in gkv_parts], axis=2)

    m_mine = jnp.dot(att, w_mine, preferred_element_type=F32).astype(BF16)
    m_mate = jnp.dot(att, w_mate, preferred_element_type=F32).astype(BF16)
    mixed = jnp.concatenate(
        [jnp.where(first, m_mine, m_mate), jnp.where(first, m_mate, m_mine)], axis=1
    )
    return (
        mixed.reshape(upstream.shape),
        grad_q.reshape(queries.shape),
        grad_kv.reshape(keys_values.shape),
        grad_weight,
    )


def solution(mesh):
    fine = Mesh(mesh.devices.reshape(2, 2, 2, 8, 4), ("xl", "xh", "co", "z", "y"))
    wa = ("z", "y")
    ha = ("xh", "co")
    return jax.shard_map(
        per_device,
        mesh=fine,
        in_specs=(
            P(wa, "xl", ha, None, None),
            P(None, wa, "xl", ha, None, None),
            P(wa, "xl", ha, None, None),
            P(None, wa, None),
            P(),
        ),
        out_specs=(
            P(wa, "xl", ha, None, None),
            P(wa, "xl", ha, None, None),
            P(None, wa, "xl", ha, None, None),
            P(wa, None),
        ),
        check_vma=False,
    )
```

```python
import functools

import jax
import jax.numpy as jnp
from jax import lax
from jax.experimental import pallas as pl
from jax.experimental.pallas import tpu as pltpu
from jax.sharding import Mesh, PartitionSpec as P

HEADS = 12
HEAD_DIM = 128
SCALE = HEAD_DIM ** (-0.5)
TILE = 192
SLOTS = 4
PER_STEP = 3
GROUP = PER_STEP * HEAD_DIM
NT = (((1,), (1,)), ((), ()))
TN = (((0,), (0,)), ((), ()))
F32 = jnp.float32
BF16 = jnp.bfloat16
PARAMS = pltpu.CompilerParams(vmem_limit_bytes=40 * 1024 * 1024)


def window_of(refs, which, cols):
    return jnp.concatenate([ref[which, :, cols] for ref in refs], axis=0)


def probs_of(q, k, bound):
    scores = lax.dot_general(q, k, NT, preferred_element_type=F32)
    column = lax.broadcasted_iota(jnp.int32, scores.shape, 1)
    scores = jnp.where(column < bound, scores, -1e30)
    top = jnp.max(scores, axis=1, keepdims=True)
    weights = jnp.exp((scores - top) * SCALE)
    return weights * (1.0 / jnp.sum(weights, axis=1, keepdims=True))


def forward_kernel(bound_ref, q_ref, own_ref, time_ref, core_ref, cross_ref, out_ref):
    kv = (own_ref, time_ref, core_ref, cross_ref)
    for h in range(PER_STEP):
        cols = slice(h * HEAD_DIM, (h + 1) * HEAD_DIM)
        k = window_of(kv, 0, cols)
        v = window_of(kv, 1, cols)
        probs = probs_of(q_ref[:, cols], k, bound_ref[0])
        out = jnp.dot(probs.astype(BF16), v, preferred_element_type=F32)
        out_ref[:, cols] = out.astype(BF16)


def backward_kernel(group, scalar_ref, q_ref, own_ref, time_ref, core_ref, cross_ref, att_ref, *rest):
    pieces, gq_ref, outs, d_ref = rest[:4], rest[4], rest[5:9], rest[9]
    kv = (own_ref, time_ref, core_ref, cross_ref)
    at = lax.rem(group + pl.program_id(0) - scalar_ref[1] + 4, 4)
    for i in range(4):

        @pl.when(at == i)
        def _():
            d_ref[...] = pieces[i][...]

    for h in range(PER_STEP):
        cols = slice(h * HEAD_DIM, (h + 1) * HEAD_DIM)
        q = q_ref[:, cols]
        k = window_of(kv, 0, cols)
        v = window_of(kv, 1, cols)
        d = d_ref[:, cols]
        probs = probs_of(q, k, scalar_ref[0])
        delta = jnp.sum(d.astype(F32) * att_ref[:, cols].astype(F32), axis=1, keepdims=True)
        d_probs = lax.dot_general(d, v, NT, preferred_element_type=F32)
        d_scores = (probs * (d_probs - delta)).astype(BF16)
        value_terms = lax.dot_general(probs.astype(BF16), d, TN, preferred_element_type=F32)
        key_terms = lax.dot_general(d_scores, q, TN, preferred_element_type=F32) * SCALE
        gq = jnp.dot(d_scores, k, preferred_element_type=F32) * SCALE
        gq_ref[:, cols] = gq.astype(BF16)
        for s, ref in enumerate(outs):
            rows = slice(s * TILE, (s + 1) * TILE)
            ref[0, :, cols] = key_terms[rows].astype(ref.dtype)
            ref[1, :, cols] = value_terms[rows].astype(ref.dtype)


def flat_spec(first):
    return pl.BlockSpec((TILE, GROUP), lambda i, b: (0, i + first))


def pair_spec(first):
    return pl.BlockSpec((2, TILE, GROUP), lambda i, b: (0, 0, i + first))


def whole(shape):
    return pl.BlockSpec(shape, lambda *_: (0,) * len(shape))


def attention_forward(scalars, q, kvs, first, groups):
    return pl.pallas_call(
        forward_kernel,
        grid_spec=pltpu.PrefetchScalarGridSpec(
            num_scalar_prefetch=1,
            grid=(groups,),
            in_specs=[flat_spec(first), pair_spec(first), pair_spec(0), pair_spec(first), pair_spec(0)],
            out_specs=flat_spec(0),
        ),
        out_shape=jax.ShapeDtypeStruct((TILE, groups * GROUP), BF16),
        compiler_params=PARAMS,
        cost_estimate=pl.CostEstimate(
            flops=4 * groups * TILE * SLOTS * TILE * GROUP,
            bytes_accessed=20 * TILE * groups * GROUP,
            transcendentals=groups * PER_STEP * TILE * SLOTS * TILE,
        ),
    )(scalars, q, *kvs)


def attention_backward(scalars, q, kvs, att, pieces, first, groups):
    width = groups * GROUP
    return pl.pallas_call(
        functools.partial(backward_kernel, first),
        grid_spec=pltpu.PrefetchScalarGridSpec(
            num_scalar_prefetch=1,
            grid=(groups,),
            in_specs=[flat_spec(first), pair_spec(first), pair_spec(0), pair_spec(first), pair_spec(0), flat_spec(0)]
            + [whole((TILE, GROUP))] * 4,
            out_specs=[flat_spec(0)] + [pair_spec(0)] * 4,
            scratch_shapes=[pltpu.VMEM((TILE, GROUP), BF16)],
        ),
        out_shape=[jax.ShapeDtypeStruct((TILE, width), BF16), jax.ShapeDtypeStruct((2, TILE, width), F32)]
        + [jax.ShapeDtypeStruct((2, TILE, width), BF16)] * 3,
        compiler_params=PARAMS,
        cost_estimate=pl.CostEstimate(
            flops=12 * groups * TILE * SLOTS * TILE * GROUP,
            bytes_accessed=48 * TILE * width,
            transcendentals=groups * PER_STEP * TILE * SLOTS * TILE,
        ),
    )(scalars, q, *kvs, att, *pieces)


def ordered_kernel(scalar_ref, *refs):
    pieces, out_ref = refs[:-1], refs[-1]
    rows = pieces[0].shape[0]
    count = len(pieces)
    for k, piece in enumerate(pieces):
        row = pl.multiple_of(lax.rem(scalar_ref[2] - k + count, count) * rows, 16)
        out_ref[pl.ds(row, rows), :] = piece[...]


def ordered(scalars, pieces):
    rows, cols = pieces[0].shape
    return pl.pallas_call(
        ordered_kernel,
        grid_spec=pltpu.PrefetchScalarGridSpec(
            num_scalar_prefetch=1,
            grid=(1,),
            in_specs=[whole((rows, cols))] * len(pieces),
            out_specs=whole((rows * len(pieces), cols)),
        ),
        out_shape=jax.ShapeDtypeStruct((rows * len(pieces), cols), BF16),
        compiler_params=PARAMS,
        cost_estimate=pl.CostEstimate(
            flops=0, bytes_accessed=4 * rows * cols * len(pieces), transcendentals=0
        ),
    )(scalars, *pieces)


def d_attention_kernel(scalar_ref, *refs):
    ups, mine_ref, mate_ref, outs, weight_ref = refs[:4], refs[4], refs[5], refs[6:10], refs[10]
    co = scalar_ref[3]
    half = mine_ref.shape[1]
    for side, ref in enumerate((mine_ref, mate_ref)):
        column = pl.multiple_of((co if side == 0 else 1 - co) * half, 128)
        weight_ref[:, pl.ds(column, half)] = ref[...]
    for up, out in zip(ups, outs):
        out[...] = lax.dot_general(
            up[...], weight_ref[...], NT, preferred_element_type=F32
        ).astype(BF16)


def d_attention(scalars, ups, w_mine, w_mate):
    dout = ups[0].shape[1]
    return pl.pallas_call(
        d_attention_kernel,
        grid_spec=pltpu.PrefetchScalarGridSpec(
            num_scalar_prefetch=1,
            grid=(1,),
            in_specs=[whole((TILE, dout))] * 4 + [whole(w_mine.shape)] * 2,
            out_specs=[whole((TILE, GROUP))] * 4 + [whole((GROUP, dout))],
        ),
        out_shape=[jax.ShapeDtypeStruct((TILE, GROUP), BF16)] * 4
        + [jax.ShapeDtypeStruct((GROUP, dout), BF16)],
        compiler_params=PARAMS,
        cost_estimate=pl.CostEstimate(
            flops=8 * TILE * GROUP * dout, bytes_accessed=8 * TILE * dout + 4 * GROUP * dout, transcendentals=0
        ),
    )(scalars, *ups, w_mine, w_mate)


def gradient_kernel(scalar_ref, *refs):
    atts, ups, out_ref = refs[:4], refs[4:8], refs[8]
    total = lax.dot_general(atts[0][...], ups[0][...], TN, preferred_element_type=F32)
    for k in range(1, 4):
        total += lax.dot_general(atts[k][...], ups[k][...], TN, preferred_element_type=F32)
    out_ref[...] = total.astype(out_ref.dtype)


def weight_gradient(scalars, atts, ups, mate, kind):
    half = ups[0].shape[1] // 2
    step = 256
    steps = half // step

    def column(i, b):
        co = 1 - b[3] if mate else b[3]
        return (0, co * steps + i)

    return pl.pallas_call(
        gradient_kernel,
        grid_spec=pltpu.PrefetchScalarGridSpec(
            num_scalar_prefetch=1,
            grid=(steps,),
            in_specs=[whole((TILE, GROUP))] * 4 + [pl.BlockSpec((TILE, step), column)] * 4,
            out_specs=pl.BlockSpec((GROUP, step), lambda i, b: (0, i)),
        ),
        out_shape=jax.ShapeDtypeStruct((GROUP, half), kind),
        compiler_params=PARAMS,
        cost_estimate=pl.CostEstimate(
            flops=8 * TILE * GROUP * half, bytes_accessed=8 * TILE * (GROUP + half), transcendentals=0
        ),
    )(scalars, *atts, *ups)


def mixed_kernel(*refs):
    atts, weight_ref, outs = refs[:4], refs[4], refs[5:]
    for att, out in zip(atts, outs):
        out[...] = jnp.dot(att[...], weight_ref[...], preferred_element_type=F32).astype(out.dtype)


def mixed_parts(atts, weight):
    dout = weight.shape[1]
    step = 512
    return pl.pallas_call(
        mixed_kernel,
        grid=(dout // step,),
        in_specs=[whole((TILE, GROUP))] * 4 + [pl.BlockSpec((GROUP, step), lambda i: (0, i))],
        out_specs=[pl.BlockSpec((TILE, step), lambda i: (0, i))] * 4,
        out_shape=[jax.ShapeDtypeStruct((TILE, dout), F32)]
        + [jax.ShapeDtypeStruct((TILE, dout), BF16)] * 3,
        compiler_params=PARAMS,
        cost_estimate=pl.CostEstimate(
            flops=8 * TILE * GROUP * dout, bytes_accessed=10 * TILE * dout, transcendentals=0
        ),
    )(*atts, weight)


SWAP = [(0, 1), (1, 0)]
CROSS = [(1, 2), (2, 1)]


def shifted(x, axis, by):
    count = lax.axis_size(axis)
    return lax.ppermute(x, axis, [(i, (i + by) % count) for i in range(count)])


def per_device(queries, keys_values, upstream, out_weight, block_pick):
    width = queries.shape[4]
    dout = upstream.shape[4]
    half = dout // 2
    rows = out_weight.shape[1]
    ny = lax.axis_size("y")
    nz = lax.axis_size("z")
    wa = ("z", "y")
    y = lax.axis_index("y")
    z = lax.axis_index("z")
    co = lax.axis_index("co")
    first = co == 0
    q = queries.reshape(TILE, width)
    kv = keys_values.reshape(2, TILE, width)
    up = upstream.reshape(TILE, dout)

    has_cross = lax.axis_index("xh") != co
    bound = jnp.where(has_cross, SLOTS * TILE, (SLOTS - 1) * TILE)
    scalars = jnp.stack([bound, y, z, co]).astype(jnp.int32)

    parts = 2
    groups = HEADS // PER_STEP // parts
    part = groups * GROUP
    pieces = [lax.slice_in_dim(kv, c * part, (c + 1) * part, axis=2) for c in range(parts)]
    from_core = lax.ppermute(kv, "co", SWAP)
    kvs = []
    for piece in pieces:
        from_time = lax.ppermute(piece, "xl", SWAP)
        from_cross = lax.ppermute(piece, ("xh", "co"), CROSS)
        kvs.append((kv, from_time, from_core, from_cross))

    panel = lax.dynamic_slice(out_weight, (block_pick[0], 0, co * half), (1, rows, half))[0]
    w_pieces = [
        lax.ppermute(panel, wa, [(s, ny * ((s + k) % nz) + s // nz) for s in range(nz * ny)])
        for k in range(nz)
    ]
    w_mine = ordered(scalars, w_pieces)
    ups = [up] + [shifted(up, "y", k) for k in range(1, ny)]
    w_mate = lax.ppermute(w_mine, "co", SWAP)
    *d_parts, w_rows = d_attention(scalars, ups, w_mine, w_mate)
    d_pieces = d_parts[:1] + [shifted(d_parts[k], "y", -k) for k in range(1, ny)]

    att_parts = [
        attention_forward(scalars, q, kvs[c], c * groups, groups) for c in range(parts)
    ]
    att = jnp.concatenate(att_parts, axis=1)
    att_y = [
        lax.dynamic_slice_in_dim(att, lax.rem(y + k, ny) * GROUP, GROUP, axis=1) for k in range(ny)
    ]
    att_y = att_y[:1] + [shifted(att_y[k], "y", k) for k in range(1, ny)]

    grad_mate = weight_gradient(scalars, att_y, ups, True, BF16)
    grad_mine = weight_gradient(scalars, att_y, ups, False, F32)
    from_mate = lax.ppermute(grad_mate, "co", SWAP)
    grad = (grad_mine + from_mate.astype(F32)).astype(BF16).reshape(nz, rows, half)
    over_z = 0.0
    for k in range(nz):
        piece = lax.dynamic_index_in_dim(grad, lax.rem(z + k, nz), 0, keepdims=False)
        pairs = [(ny * zz + yy, nz * yy + (zz + k) % nz) for zz in range(nz) for yy in range(ny)]
        over_z = over_z + lax.ppermute(piece, wa, pairs).astype(F32)
    over_z = over_z.astype(BF16)
    x_near = lax.ppermute(over_z, "xl", SWAP)
    x_far = lax.ppermute(over_z, "xh", SWAP)
    x_both = lax.ppermute(over_z, ("xl", "xh"), [(i, 3 - i) for i in range(4)])
    mine = (over_z.astype(F32) + x_near.astype(F32)) + (x_far.astype(F32) + x_both.astype(F32))
    mate = lax.ppermute(mine, "co", SWAP)
    grad_weight = jnp.concatenate(
        [jnp.where(first, mine, mate), jnp.where(first, mate, mine)], axis=1
    )

    gq_parts, gkv_parts = [], []
    for c in range(parts):
        gq, own, to_time, to_core, to_cross = attention_backward(
            scalars, q, kvs[c], att_parts[c], d_pieces, c * groups, groups
        )
        gq_parts.append(gq)
        terms = (
            lax.ppermute(to_time, "xl", SWAP),
            lax.ppermute(to_cross, ("xh", "co"), CROSS),
            lax.ppermute(to_core, "co", SWAP),
        )
        gkv_parts.append(own + sum(t.astype(F32) for t in terms))
    grad_q = jnp.concatenate(gq_parts, axis=1)
    grad_kv = jnp.concatenate([p.astype(BF16) for p in gkv_parts], axis=2)

    m_mine, *m_others = mixed_parts(att_y, w_rows)
    for k in range(1, ny):
        m_mine = m_mine + shifted(m_others[k - 1], "y", -k).astype(F32)
    return (
        m_mine.astype(BF16).reshape(upstream.shape),
        grad_q.reshape(queries.shape),
        grad_kv.reshape(keys_values.shape),
        grad_weight,
    )


def solution(mesh):
    fine = Mesh(mesh.devices.reshape(2, 2, 2, 8, 4), ("xl", "xh", "co", "z", "y"))
    wa = ("z", "y")
    ha = ("xh", "co")
    return jax.shard_map(
        per_device,
        mesh=fine,
        in_specs=(
            P(wa, "xl", ha, None, None),
            P(None, wa, "xl", ha, None, None),
            P(wa, "xl", ha, None, None),
            P(None, wa, None),
            P(),
        ),
        out_specs=(
            P(wa, "xl", ha, None, None),
            P(wa, "xl", ha, None, None),
            P(None, wa, "xl", ha, None, None),
            P(wa, None),
        ),
        check_vma=False,
    )
```

```python
import jax
import jax.numpy as jnp
from jax import lax
from jax.experimental import pallas as pl
from jax.experimental.pallas import tpu as pltpu
from jax.sharding import Mesh, PartitionSpec as P

HEADS = 12
HEAD_DIM = 128
SCALE = HEAD_DIM ** (-0.5)
TILE = 192
SLOTS = 4
PER_STEP = 3
GROUP = PER_STEP * HEAD_DIM
ROWS = 48
NY = 4
PAD = 256
MASKED = 512
NT = (((1,), (1,)), ((), ()))
TN = (((0,), (0,)), ((), ()))
F32 = jnp.float32
BF16 = jnp.bfloat16
PARAMS = pltpu.CompilerParams(vmem_limit_bytes=56 * 1024 * 1024)


def window_of(refs, which, cols):
    return jnp.concatenate([ref[which, :, cols] for ref in refs], axis=0)


def probs_of(q, k, bound):
    scores = lax.dot_general(q, k, NT, preferred_element_type=F32)
    tail = scores[:, MASKED:]
    column = lax.broadcasted_iota(jnp.int32, tail.shape, 1)
    tail = jnp.where(column + MASKED < bound, tail, -1e30)
    scores = jnp.concatenate([scores[:, :MASKED], tail], axis=1)
    top = jnp.max(scores, axis=1, keepdims=True)
    weights = jnp.exp((scores - top) * SCALE)
    return weights * (1.0 / jnp.sum(weights, axis=1, keepdims=True))


def forward_kernel(scalar_ref, q_ref, own_ref, time_ref, core_ref, cross_ref, out_ref, out_t_ref, probs_ref):
    kv = (own_ref, time_ref, core_ref, cross_ref)
    for h in range(PER_STEP):
        cols = slice(h * HEAD_DIM, (h + 1) * HEAD_DIM)
        k = window_of(kv, 0, cols)
        v = window_of(kv, 1, cols)
        probs = probs_of(q_ref[:, cols], k, scalar_ref[0])
        probs_b = probs.astype(BF16)
        probs_ref[h] = probs_b
        out = jnp.dot(probs_b, v, preferred_element_type=F32)
        out_ref[:, cols] = out.astype(BF16)
    flipped = out_ref[...].astype(F32).T.astype(BF16)
    for b in range(GROUP // ROWS):
        block = flipped[b * ROWS : (b + 1) * ROWS]
        out_t_ref[b % NY, b // NY] = jnp.concatenate([block, jnp.zeros((ROWS, PAD - TILE), BF16)], axis=1)


def backward_kernel(
    scalar_ref, q_ref, own_ref, time_ref, core_ref, cross_ref, att_ref, d_ref, probs_ref,
    gq_ref, g_own_ref, g_time_ref, g_core_ref, g_cross_ref,
):
    kv = (own_ref, time_ref, core_ref, cross_ref)
    outs = (g_own_ref, g_time_ref, g_core_ref, g_cross_ref)
    flipped = jnp.concatenate(
        [d_ref[b % NY, b // NY] for b in range(GROUP // ROWS)], axis=0
    )
    d_all = flipped.astype(F32).T[:TILE].astype(BF16)
    for h in range(PER_STEP):
        cols = slice(h * HEAD_DIM, (h + 1) * HEAD_DIM)
        q = q_ref[:, cols]
        k = window_of(kv, 0, cols)
        v = window_of(kv, 1, cols)
        d = d_all[:, cols]
        probs = probs_ref[h]
        delta = jnp.sum(d.astype(F32) * att_ref[:, cols].astype(F32), axis=1, keepdims=True)
        d_probs = lax.dot_general(d, v, NT, preferred_element_type=F32)
        d_scores = (probs.astype(F32) * (d_probs - delta)).astype(BF16)
        value_terms = lax.dot_general(probs, d, TN, preferred_element_type=F32)
        key_terms = lax.dot_general(d_scores, q, TN, preferred_element_type=F32) * SCALE
        gq = jnp.dot(d_scores, k, preferred_element_type=F32) * SCALE
        gq_ref[:, cols] = gq.astype(BF16)
        for s, ref in enumerate(outs):
            rows = slice(s * TILE, (s + 1) * TILE)
            ref[0, :, cols] = key_terms[rows].astype(ref.dtype)
            ref[1, :, cols] = value_terms[rows].astype(ref.dtype)


def flat_spec(first):
    return pl.BlockSpec((TILE, GROUP), lambda i, b: (0, i + first))


def pair_spec(first):
    return pl.BlockSpec((2, TILE, GROUP), lambda i, b: (0, 0, i + first))


def turned_spec(first):
    return pl.BlockSpec((NY, GROUP // ROWS // NY, ROWS, PAD), lambda i, b: (0, i + first, 0, 0))


def probs_spec(first):
    return pl.BlockSpec((PER_STEP, TILE, SLOTS * TILE), lambda i, b: (i + first, 0, 0))


def whole(shape):
    return pl.BlockSpec(shape, lambda *_: (0,) * len(shape))


def attention_forward(scalars, q, kvs):
    groups = HEADS // PER_STEP
    return pl.pallas_call(
        forward_kernel,
        grid_spec=pltpu.PrefetchScalarGridSpec(
            num_scalar_prefetch=1,
            grid=(groups,),
            in_specs=[flat_spec(0)] + [pair_spec(0)] * 4,
            out_specs=[flat_spec(0), turned_spec(0), probs_spec(0)],
        ),
        out_shape=[
            jax.ShapeDtypeStruct((TILE, groups * GROUP), BF16),
            jax.ShapeDtypeStruct((NY, groups * GROUP // ROWS // NY, ROWS, PAD), BF16),
            jax.ShapeDtypeStruct((HEADS, TILE, SLOTS * TILE), BF16),
        ],
        compiler_params=PARAMS,
        cost_estimate=pl.CostEstimate(
            flops=4 * groups * TILE * SLOTS * TILE * GROUP,
            bytes_accessed=20 * TILE * groups * GROUP,
            transcendentals=groups * PER_STEP * TILE * SLOTS * TILE,
        ),
    )(scalars, q, *kvs)


def attention_backward(scalars, q, kvs, att, d, probs, first, groups):
    width = groups * GROUP
    return pl.pallas_call(
        backward_kernel,
        grid_spec=pltpu.PrefetchScalarGridSpec(
            num_scalar_prefetch=1,
            grid=(groups,),
            in_specs=[flat_spec(first)] + [pair_spec(first)] * 4 + [flat_spec(first), turned_spec(first), probs_spec(first)],
            out_specs=[flat_spec(0)] + [pair_spec(0)] * 4,
        ),
        out_shape=[jax.ShapeDtypeStruct((TILE, width), BF16)]
        + [jax.ShapeDtypeStruct((2, TILE, width), BF16)] * 4,
        compiler_params=PARAMS,
        cost_estimate=pl.CostEstimate(
            flops=12 * groups * TILE * SLOTS * TILE * GROUP,
            bytes_accessed=48 * TILE * width,
            transcendentals=groups * PER_STEP * TILE * SLOTS * TILE,
        ),
    )(scalars, q, *kvs, att, d, probs)


def d_attention_kernel(scalar_ref, up_ref, mine_ref, mate_ref, out_ref, weight_ref):
    half = mine_ref.shape[1]

    @pl.when(pl.program_id(0) == 0)
    def _():
        for side, ref in enumerate((mine_ref, mate_ref)):
            co = scalar_ref[1] if side == 0 else 1 - scalar_ref[1]
            weight_ref[:, pl.ds(pl.multiple_of(co * half, 128), half)] = ref[...]

    out = lax.dot_general(weight_ref[...], up_ref[0], NT, preferred_element_type=F32)
    out_ref[0] = jnp.concatenate(
        [out.astype(BF16), jnp.zeros((out.shape[0], PAD - TILE), BF16)], axis=1
    )


def d_attention(scalars, ups, w_mine, w_mate):
    dout = ups.shape[2]
    rows = w_mine.shape[0]
    return pl.pallas_call(
        d_attention_kernel,
        grid_spec=pltpu.PrefetchScalarGridSpec(
            num_scalar_prefetch=1,
            grid=(NY,),
            in_specs=[pl.BlockSpec((1, TILE, dout), lambda i, b: (i, 0, 0))] + [whole(w_mine.shape)] * 2,
            out_specs=[pl.BlockSpec((1, rows, PAD), lambda i, b: (i, 0, 0)), whole((rows, dout))],
        ),
        out_shape=[
            jax.ShapeDtypeStruct((NY, rows, PAD), BF16),
            jax.ShapeDtypeStruct((rows, dout), BF16),
        ],
        compiler_params=PARAMS,
        cost_estimate=pl.CostEstimate(
            flops=8 * TILE * rows * dout, bytes_accessed=8 * TILE * dout + 4 * rows * dout, transcendentals=0
        ),
    )(scalars, ups, w_mine, w_mate)


def gradient_kernel(scalar_ref, att_ref, mine_ref, mate_ref, out_mine_ref, out_mate_ref):
    for up_ref, out_ref in ((mine_ref, out_mine_ref), (mate_ref, out_mate_ref)):
        total = jnp.dot(att_ref[0][:, :TILE], up_ref[0], preferred_element_type=F32)
        for k in range(1, NY):
            total += jnp.dot(att_ref[k][:, :TILE], up_ref[k], preferred_element_type=F32)
        out_ref[...] = total.astype(out_ref.dtype)


def weight_gradient(scalars, atts, ups):
    half = ups.shape[2] // 2
    rows = atts.shape[1]
    step = 256
    steps = half // step
    return pl.pallas_call(
        gradient_kernel,
        grid_spec=pltpu.PrefetchScalarGridSpec(
            num_scalar_prefetch=1,
            grid=(steps,),
            in_specs=[
                whole(atts.shape),
                pl.BlockSpec((NY, TILE, step), lambda i, b: (0, 0, b[1] * steps + i)),
                pl.BlockSpec((NY, TILE, step), lambda i, b: (0, 0, (1 - b[1]) * steps + i)),
            ],
            out_specs=[pl.BlockSpec((rows, step), lambda i, b: (0, i))] * 2,
        ),
        out_shape=[jax.ShapeDtypeStruct((rows, half), BF16)] * 2,
        compiler_params=PARAMS,
        cost_estimate=pl.CostEstimate(
            flops=16 * TILE * rows * half, bytes_accessed=16 * TILE * (rows + half), transcendentals=0
        ),
    )(scalars, atts, ups, ups)


def mixed_kernel(att_ref, weight_ref, out_ref):
    att = att_ref[0][:, :TILE]
    out_ref[0] = lax.dot_general(att, weight_ref[...], TN, preferred_element_type=F32).astype(BF16)


def mixed_parts(atts, weight):
    rows, dout = weight.shape
    return pl.pallas_call(
        mixed_kernel,
        grid=(NY,),
        in_specs=[pl.BlockSpec((1, rows, PAD), lambda i: (i, 0, 0)), whole((rows, dout))],
        out_specs=pl.BlockSpec((1, TILE, dout), lambda i: (i, 0, 0)),
        out_shape=jax.ShapeDtypeStruct((NY, TILE, dout), BF16),
        compiler_params=PARAMS,
        cost_estimate=pl.CostEstimate(
            flops=8 * TILE * rows * dout, bytes_accessed=10 * TILE * dout, transcendentals=0
        ),
    )(atts, weight)


SWAP = [(0, 1), (1, 0)]
CROSS = [(1, 2), (2, 1)]


def swapped(x, axis):
    return lax.all_to_all(x, axis, split_axis=0, concat_axis=0, tiled=True)


def per_device(queries, keys_values, upstream, out_weight, block_pick):
    width = queries.shape[4]
    dout = upstream.shape[4]
    half = dout // 2
    rows = out_weight.shape[1]
    ny = lax.axis_size("y")
    nz = lax.axis_size("z")
    co = lax.axis_index("co")
    first = co == 0
    q = queries.reshape(TILE, width)
    kv = keys_values.reshape(2, TILE, width)
    up = upstream.reshape(TILE, dout)

    has_cross = lax.axis_index("xh") != co
    bound = jnp.where(has_cross, SLOTS * TILE, (SLOTS - 1) * TILE)
    scalars = jnp.stack([bound, co]).astype(jnp.int32)

    from_time = lax.ppermute(kv, "xl", SWAP)
    from_cross = lax.ppermute(kv, ("xh", "co"), CROSS)
    from_core = lax.ppermute(kv, "co", SWAP)
    kvs = (kv, from_time, from_core, from_cross)

    panel = lax.dynamic_slice(out_weight, (block_pick[0], 0, co * half), (1, rows, half))
    w_mine = swapped(jnp.broadcast_to(panel, (nz, rows, half)), "z").reshape(nz * rows, half)
    ups = swapped(jnp.broadcast_to(up[None], (ny, TILE, dout)), "y")
    w_mate = lax.ppermute(w_mine, "co", SWAP)
    d_parts, w_rows = d_attention(scalars, ups, w_mine, w_mate)
    d_turned = swapped(d_parts, "y").reshape(ny, nz, rows, PAD)

    kvs, d_parts = lax.optimization_barrier((kvs, d_parts))
    att, att_turned, probs = attention_forward(scalars, q, kvs)
    atts = swapped(att_turned.reshape(ny, nz * rows, PAD), "y")

    parts = 2
    groups = HEADS // PER_STEP // parts

    def backward(c):
        gq, own, to_time, to_core, to_cross = attention_backward(
            scalars, q, kvs, att, d_turned, probs, c * groups, groups
        )
        terms = (
            lax.ppermute(to_time, "xl", SWAP),
            lax.ppermute(to_cross, ("xh", "co"), CROSS),
            lax.ppermute(to_core, "co", SWAP),
        )
        return gq, own.astype(F32) + sum(t.astype(F32) for t in terms)

    gq_0, gkv_0 = backward(0)
    atts, gq_0 = lax.optimization_barrier((atts, gq_0))
    grad_mine, grad_mate = weight_gradient(scalars, atts, ups)
    from_mate = lax.ppermute(grad_mate, "co", SWAP)
    atts, w_rows, grad_mine = lax.optimization_barrier((atts, w_rows, grad_mine))
    mixed = mixed_parts(atts, w_rows)
    grad = (grad_mine.astype(F32) + from_mate.astype(F32)).astype(BF16).reshape(nz, rows, half)
    probs, grad, mixed = lax.optimization_barrier((probs, grad, mixed))
    gq_1, gkv_1 = backward(1)
    gq_parts, gkv_parts = (gq_0, gq_1), (gkv_0, gkv_1)
    over_z = jnp.sum(swapped(grad, "z").astype(F32), axis=0).astype(BF16)
    x_near = lax.ppermute(over_z, "xl", SWAP)
    x_far = lax.ppermute(over_z, "xh", SWAP)
    x_both = lax.ppermute(over_z, ("xl", "xh"), [(i, 3 - i) for i in range(4)])
    mine = (over_z.astype(F32) + x_near.astype(F32)) + (x_far.astype(F32) + x_both.astype(F32))
    mate = lax.ppermute(mine, "co", SWAP)
    grad_weight = jnp.concatenate(
        [jnp.where(first, mine, mate), jnp.where(first, mate, mine)], axis=1
    )

    mixed = jnp.sum(swapped(mixed, "y").astype(F32), axis=0).astype(BF16)
    grad_q = jnp.concatenate(gq_parts, axis=1)
    grad_kv = jnp.concatenate([p.astype(BF16) for p in gkv_parts], axis=2)
    return (
        mixed.reshape(upstream.shape),
        grad_q.reshape(queries.shape),
        grad_kv.reshape(keys_values.shape),
        grad_weight,
    )


def solution(mesh):
    fine = Mesh(mesh.devices.reshape(2, 2, 2, 8, 4), ("xl", "xh", "co", "z", "y"))
    wa = ("z", "y")
    ha = ("xh", "co")
    return jax.shard_map(
        per_device,
        mesh=fine,
        in_specs=(
            P(wa, "xl", ha, None, None),
            P(None, wa, "xl", ha, None, None),
            P(wa, "xl", ha, None, None),
            P(None, wa, None),
            P(),
        ),
        out_specs=(
            P(wa, "xl", ha, None, None),
            P(wa, "xl", ha, None, None),
            P(None, wa, "xl", ha, None, None),
            P(wa, None),
        ),
        check_vma=False,
    )
```

```python
import jax
import jax.numpy as jnp
from jax import lax
from jax.experimental import pallas as pl
from jax.experimental.pallas import tpu as pltpu
from jax.sharding import Mesh, PartitionSpec as P

HEADS = 12
HEAD_DIM = 128
SCALE = HEAD_DIM ** (-0.5)
TILE = 192
SLOTS = 4
PER_STEP = 3
GROUP = PER_STEP * HEAD_DIM
ROWS = 48
NY = 4
PAD = 256
MASKED = 512
NT = (((1,), (1,)), ((), ()))
TN = (((0,), (0,)), ((), ()))
F32 = jnp.float32
BF16 = jnp.bfloat16
PARAMS = pltpu.CompilerParams(vmem_limit_bytes=56 * 1024 * 1024)


def window_of(refs, which, cols):
    return jnp.concatenate([ref[which, :, cols] for ref in refs], axis=0)


def probs_of(q, k, bound):
    scores = lax.dot_general(q, k, NT, preferred_element_type=F32)
    tail = scores[:, MASKED:]
    column = lax.broadcasted_iota(jnp.int32, tail.shape, 1)
    tail = jnp.where(column + MASKED < bound, tail, -1e30)
    scores = jnp.concatenate([scores[:, :MASKED], tail], axis=1)
    top = jnp.max(scores, axis=1, keepdims=True)
    weights = jnp.exp((scores - top) * SCALE)
    return weights * (1.0 / jnp.sum(weights, axis=1, keepdims=True))


def forward_kernel(scalar_ref, q_ref, own_ref, time_ref, core_ref, cross_ref, out_ref, out_t_ref, probs_ref):
    kv = (own_ref, time_ref, core_ref, cross_ref)
    for h in range(PER_STEP):
        cols = slice(h * HEAD_DIM, (h + 1) * HEAD_DIM)
        k = window_of(kv, 0, cols)
        v = window_of(kv, 1, cols)
        probs = probs_of(q_ref[:, cols], k, scalar_ref[0])
        probs_b = probs.astype(BF16)
        probs_ref[h] = probs_b
        out = jnp.dot(probs_b, v, preferred_element_type=F32)
        out_ref[:, cols] = out.astype(BF16)
    flipped = out_ref[...].astype(F32).T.astype(BF16)
    for b in range(GROUP // ROWS):
        block = flipped[b * ROWS : (b + 1) * ROWS]
        out_t_ref[b % NY, b // NY] = jnp.concatenate([block, jnp.zeros((ROWS, PAD - TILE), BF16)], axis=1)


def backward_kernel(
    scalar_ref, q_ref, own_ref, time_ref, core_ref, cross_ref, att_ref, d_ref, probs_ref,
    gq_ref, g_own_ref, g_time_ref, g_core_ref, g_cross_ref,
):
    kv = (own_ref, time_ref, core_ref, cross_ref)
    outs = (g_own_ref, g_time_ref, g_core_ref, g_cross_ref)
    flipped = jnp.concatenate(
        [d_ref[b % NY, b // NY] for b in range(GROUP // ROWS)], axis=0
    )
    d_all = flipped.astype(F32).T[:TILE].astype(BF16)
    for h in range(PER_STEP):
        cols = slice(h * HEAD_DIM, (h + 1) * HEAD_DIM)
        q = q_ref[:, cols]
        k = window_of(kv, 0, cols)
        v = window_of(kv, 1, cols)
        d = d_all[:, cols]
        probs = probs_ref[h]
        delta = jnp.sum(d.astype(F32) * att_ref[:, cols].astype(F32), axis=1, keepdims=True)
        d_probs = lax.dot_general(d, v, NT, preferred_element_type=F32)
        d_scores = (probs.astype(F32) * (d_probs - delta)).astype(BF16)
        value_terms = lax.dot_general(probs, d, TN, preferred_element_type=F32)
        key_terms = lax.dot_general(d_scores, q, TN, preferred_element_type=F32) * SCALE
        gq = jnp.dot(d_scores, k, preferred_element_type=F32) * SCALE
        gq_ref[:, cols] = gq.astype(BF16)
        for s, ref in enumerate(outs):
            rows = slice(s * TILE, (s + 1) * TILE)
            ref[0, :, cols] = key_terms[rows].astype(ref.dtype)
            ref[1, :, cols] = value_terms[rows].astype(ref.dtype)


def flat_spec(first):
    return pl.BlockSpec((TILE, GROUP), lambda i, b: (0, i + first))


def pair_spec(first):
    return pl.BlockSpec((2, TILE, GROUP), lambda i, b: (0, 0, i + first))


def turned_spec(first):
    return pl.BlockSpec((NY, GROUP // ROWS // NY, ROWS, PAD), lambda i, b: (0, i + first, 0, 0))


def probs_spec(first):
    return pl.BlockSpec((PER_STEP, TILE, SLOTS * TILE), lambda i, b: (i + first, 0, 0))


def whole(shape):
    return pl.BlockSpec(shape, lambda *_: (0,) * len(shape))


def attention_forward(scalars, q, kvs):
    groups = HEADS // PER_STEP
    return pl.pallas_call(
        forward_kernel,
        grid_spec=pltpu.PrefetchScalarGridSpec(
            num_scalar_prefetch=1,
            grid=(groups,),
            in_specs=[flat_spec(0)] + [pair_spec(0)] * 4,
            out_specs=[flat_spec(0), turned_spec(0), probs_spec(0)],
        ),
        out_shape=[
            jax.ShapeDtypeStruct((TILE, groups * GROUP), BF16),
            jax.ShapeDtypeStruct((NY, groups * GROUP // ROWS // NY, ROWS, PAD), BF16),
            jax.ShapeDtypeStruct((HEADS, TILE, SLOTS * TILE), BF16),
        ],
        compiler_params=PARAMS,
        cost_estimate=pl.CostEstimate(
            flops=4 * groups * TILE * SLOTS * TILE * GROUP,
            bytes_accessed=20 * TILE * groups * GROUP,
            transcendentals=groups * PER_STEP * TILE * SLOTS * TILE,
        ),
    )(scalars, q, *kvs)


def attention_backward(scalars, q, kvs, att, d, probs, first, groups):
    width = groups * GROUP
    return pl.pallas_call(
        backward_kernel,
        grid_spec=pltpu.PrefetchScalarGridSpec(
            num_scalar_prefetch=1,
            grid=(groups,),
            in_specs=[flat_spec(first)] + [pair_spec(first)] * 4 + [flat_spec(first), turned_spec(first), probs_spec(first)],
            out_specs=[flat_spec(0)] + [pair_spec(0)] * 4,
        ),
        out_shape=[jax.ShapeDtypeStruct((TILE, width), BF16)]
        + [jax.ShapeDtypeStruct((2, TILE, width), BF16)] * 4,
        compiler_params=PARAMS,
        cost_estimate=pl.CostEstimate(
            flops=12 * groups * TILE * SLOTS * TILE * GROUP,
            bytes_accessed=48 * TILE * width,
            transcendentals=groups * PER_STEP * TILE * SLOTS * TILE,
        ),
    )(scalars, q, *kvs, att, d, probs)


def source(scalar_ref, k):
    return lax.rem(scalar_ref[2] - k + NY, NY)


def d_attention_kernel(scalar_ref, *refs):
    ups, mine_ref, mate_ref, out_ref, weight_ref = refs[:NY], *refs[NY:]
    half = mine_ref.shape[1]
    for side, ref in enumerate((mine_ref, mate_ref)):
        co = scalar_ref[1] if side == 0 else 1 - scalar_ref[1]
        weight_ref[:, pl.ds(pl.multiple_of(co * half, 128), half)] = ref[...]
    for k, up in enumerate(ups):
        out = lax.dot_general(weight_ref[...], up[...], NT, preferred_element_type=F32)
        out_ref[source(scalar_ref, k)] = jnp.concatenate(
            [out.astype(BF16), jnp.zeros((out.shape[0], PAD - TILE), BF16)], axis=1
        )


def d_attention(scalars, ups, w_mine, w_mate):
    dout = ups[0].shape[1]
    rows = w_mine.shape[0]
    return pl.pallas_call(
        d_attention_kernel,
        grid_spec=pltpu.PrefetchScalarGridSpec(
            num_scalar_prefetch=1,
            grid=(1,),
            in_specs=[whole((TILE, dout))] * NY + [whole(w_mine.shape)] * 2,
            out_specs=[whole((NY, rows, PAD)), whole((rows, dout))],
        ),
        out_shape=[
            jax.ShapeDtypeStruct((NY, rows, PAD), BF16),
            jax.ShapeDtypeStruct((rows, dout), BF16),
        ],
        compiler_params=PARAMS,
        cost_estimate=pl.CostEstimate(
            flops=8 * TILE * rows * dout, bytes_accessed=8 * TILE * dout + 4 * rows * dout, transcendentals=0
        ),
    )(scalars, *ups, w_mine, w_mate)


def gradient_kernel(scalar_ref, att_ref, *refs):
    ups, outs = refs[: 2 * NY], refs[2 * NY :]
    for side, out_ref in enumerate(outs):
        total = 0.0
        for k in range(NY):
            att = att_ref[source(scalar_ref, k)][:, :TILE]
            total += jnp.dot(att, ups[side * NY + k][...], preferred_element_type=F32)
        out_ref[...] = total.astype(out_ref.dtype)


def weight_gradient(scalars, atts, ups):
    half = ups[0].shape[1] // 2
    rows = atts.shape[1]
    step = 256
    steps = half // step
    mine = pl.BlockSpec((TILE, step), lambda i, b: (0, b[1] * steps + i))
    mate = pl.BlockSpec((TILE, step), lambda i, b: (0, (1 - b[1]) * steps + i))
    return pl.pallas_call(
        gradient_kernel,
        grid_spec=pltpu.PrefetchScalarGridSpec(
            num_scalar_prefetch=1,
            grid=(steps,),
            in_specs=[whole(atts.shape)] + [mine] * NY + [mate] * NY,
            out_specs=[pl.BlockSpec((rows, step), lambda i, b: (0, i))] * 2,
        ),
        out_shape=[jax.ShapeDtypeStruct((rows, half), BF16)] * 2,
        compiler_params=PARAMS,
        cost_estimate=pl.CostEstimate(
            flops=16 * TILE * rows * half, bytes_accessed=16 * TILE * (rows + half), transcendentals=0
        ),
    )(scalars, atts, *ups, *ups)


def mixed_kernel(scalar_ref, att_ref, weight_ref, *outs):
    for k, out_ref in enumerate(outs):
        att = att_ref[source(scalar_ref, k)][:, :TILE]
        out = lax.dot_general(att, weight_ref[...], TN, preferred_element_type=F32)
        out_ref[...] = out.astype(BF16)


def mixed_parts(scalars, atts, weight):
    rows, dout = weight.shape
    step = 512
    return pl.pallas_call(
        mixed_kernel,
        grid_spec=pltpu.PrefetchScalarGridSpec(
            num_scalar_prefetch=1,
            grid=(dout // step,),
            in_specs=[whole(atts.shape), pl.BlockSpec((rows, step), lambda i, b: (0, i))],
            out_specs=[pl.BlockSpec((TILE, step), lambda i, b: (0, i))] * NY,
        ),
        out_shape=[jax.ShapeDtypeStruct((TILE, dout), BF16)] * NY,
        compiler_params=PARAMS,
        cost_estimate=pl.CostEstimate(
            flops=8 * TILE * rows * dout, bytes_accessed=10 * TILE * dout, transcendentals=0
        ),
    )(scalars, atts, weight)


SWAP = [(0, 1), (1, 0)]
CROSS = [(1, 2), (2, 1)]


def shifted(x, axis, by):
    count = lax.axis_size(axis)
    return lax.ppermute(x, axis, [(i, (i + by) % count) for i in range(count)])


def swapped(x, axis):
    return lax.all_to_all(x, axis, split_axis=0, concat_axis=0, tiled=True)


def per_device(queries, keys_values, upstream, out_weight, block_pick):
    width = queries.shape[4]
    dout = upstream.shape[4]
    half = dout // 2
    rows = out_weight.shape[1]
    ny = lax.axis_size("y")
    nz = lax.axis_size("z")
    co = lax.axis_index("co")
    first = co == 0
    q = queries.reshape(TILE, width)
    kv = keys_values.reshape(2, TILE, width)
    up = upstream.reshape(TILE, dout)

    has_cross = lax.axis_index("xh") != co
    bound = jnp.where(has_cross, SLOTS * TILE, (SLOTS - 1) * TILE)
    scalars = jnp.stack([bound, co, lax.axis_index("y")]).astype(jnp.int32)

    from_time = lax.ppermute(kv, "xl", SWAP)
    from_cross = lax.ppermute(kv, ("xh", "co"), CROSS)
    from_core = lax.ppermute(kv, "co", SWAP)
    kvs = (kv, from_time, from_core, from_cross)

    panel = lax.dynamic_slice(out_weight, (block_pick[0], 0, co * half), (1, rows, half))
    w_mine = swapped(jnp.broadcast_to(panel, (nz, rows, half)), "z").reshape(nz * rows, half)
    ups = [up] + [shifted(up, "y", k) for k in (1, 2, 3)]
    w_mate = lax.ppermute(w_mine, "co", SWAP)
    d_parts, w_rows = d_attention(scalars, ups, w_mine, w_mate)
    d_turned = swapped(d_parts, "y").reshape(ny, nz, rows, PAD)

    kvs, d_parts = lax.optimization_barrier((kvs, d_parts))
    att, att_turned, probs = attention_forward(scalars, q, kvs)
    atts = swapped(att_turned.reshape(ny, nz * rows, PAD), "y")

    parts = 2
    groups = HEADS // PER_STEP // parts

    def backward(c):
        gq, own, to_time, to_core, to_cross = attention_backward(
            scalars, q, kvs, att, d_turned, probs, c * groups, groups
        )
        terms = (
            lax.ppermute(to_time, "xl", SWAP),
            lax.ppermute(to_cross, ("xh", "co"), CROSS),
            lax.ppermute(to_core, "co", SWAP),
        )
        return gq, own, terms

    gq_0, own_0, terms_0 = backward(0)
    atts, gq_0 = lax.optimization_barrier((atts, gq_0))
    grad_mine, grad_mate = weight_gradient(scalars, atts, ups)
    from_mate = lax.ppermute(grad_mate, "co", SWAP)
    atts, w_rows, grad_mine = lax.optimization_barrier((atts, w_rows, grad_mine))
    mixed = mixed_parts(scalars, atts, w_rows)
    grad = (grad_mine.astype(F32) + from_mate.astype(F32)).astype(BF16).reshape(nz, rows, half)
    probs, grad, mixed, terms_0 = lax.optimization_barrier((probs, grad, mixed, terms_0))
    gq_1, own_1, terms_1 = backward(1)
    gkv_parts = [
        own.astype(F32) + sum(t.astype(F32) for t in terms)
        for own, terms in ((own_0, terms_0), (own_1, terms_1))
    ]
    gq_parts = (gq_0, gq_1)
    over_z = jnp.sum(swapped(grad, "z").astype(F32), axis=0).astype(BF16)
    x_near = lax.ppermute(over_z, "xl", SWAP)
    x_far = lax.ppermute(over_z, "xh", SWAP)
    x_both = lax.ppermute(over_z, ("xl", "xh"), [(i, 3 - i) for i in range(4)])
    mine = (over_z.astype(F32) + x_near.astype(F32)) + (x_far.astype(F32) + x_both.astype(F32))
    mate = lax.ppermute(mine, "co", SWAP)
    grad_weight = jnp.concatenate(
        [jnp.where(first, mine, mate), jnp.where(first, mate, mine)], axis=1
    )

    back = [shifted(mixed[k], "y", -k).astype(F32) for k in (1, 2, 3)]
    mixed = (mixed[0].astype(F32) + sum(back)).astype(BF16)
    grad_q = jnp.concatenate(gq_parts, axis=1)
    grad_kv = jnp.concatenate([p.astype(BF16) for p in gkv_parts], axis=2)
    return (
        mixed.reshape(upstream.shape),
        grad_q.reshape(queries.shape),
        grad_kv.reshape(keys_values.shape),
        grad_weight,
    )


def solution(mesh):
    fine = Mesh(mesh.devices.reshape(2, 2, 2, 8, 4), ("xl", "xh", "co", "z", "y"))
    wa = ("z", "y")
    ha = ("xh", "co")
    return jax.shard_map(
        per_device,
        mesh=fine,
        in_specs=(
            P(wa, "xl", ha, None, None),
            P(None, wa, "xl", ha, None, None),
            P(wa, "xl", ha, None, None),
            P(None, wa, None),
            P(),
        ),
        out_specs=(
            P(wa, "xl", ha, None, None),
            P(wa, "xl", ha, None, None),
            P(None, wa, "xl", ha, None, None),
            P(wa, None),
        ),
        check_vma=False,
    )
```

```python
import jax
import jax.numpy as jnp
from jax import lax
from jax.experimental import pallas as pl
from jax.experimental.pallas import tpu as pltpu
from jax.sharding import Mesh, PartitionSpec as P

HEADS = 12
HEAD_DIM = 128
SCALE = HEAD_DIM ** (-0.5)
LOG2E = 1.4426950408889634
TILE = 192
SLOTS = 4
PER_STEP = 3
GROUP = PER_STEP * HEAD_DIM
ROWS = 48
NY = 4
PAD = 256
MASKED = 512
NT = (((1,), (1,)), ((), ()))
TN = (((0,), (0,)), ((), ()))
F32 = jnp.float32
BF16 = jnp.bfloat16
LIGHT = pl.CostEstimate(flops=1000, bytes_accessed=1000, transcendentals=0)
PARAMS = pltpu.CompilerParams(vmem_limit_bytes=56 * 1024 * 1024)


def window_of(refs, which, cols):
    return jnp.concatenate([ref[which, :, cols] for ref in refs], axis=0)


def probs_of(scores, bound):
    tail = scores[:, MASKED:]
    column = lax.broadcasted_iota(jnp.int32, tail.shape, 1)
    tail = jnp.where(column + MASKED < bound, tail, -1e30)
    scores = jnp.concatenate([scores[:, :MASKED], tail], axis=1)
    top = jnp.max(scores, axis=1, keepdims=True)
    weights = jnp.exp2((scores - top) * (SCALE * LOG2E))
    return weights * (1.0 / jnp.sum(weights, axis=1, keepdims=True))


def head_cols(h):
    return slice(h * HEAD_DIM, (h + 1) * HEAD_DIM)


def forward_kernel(scalar_ref, q_ref, own_ref, time_ref, core_ref, cross_ref, out_ref, out_t_ref, probs_ref):
    kv = (own_ref, time_ref, core_ref, cross_ref)
    scores = [
        lax.dot_general(
            q_ref[:, head_cols(h)], window_of(kv, 0, head_cols(h)), NT, preferred_element_type=F32
        )
        for h in range(PER_STEP)
    ]
    outs = []
    for h in range(PER_STEP):
        probs_b = probs_of(scores[h], scalar_ref[0]).astype(BF16)
        probs_ref[h] = probs_b
        v = window_of(kv, 1, head_cols(h))
        outs.append(jnp.dot(probs_b, v, preferred_element_type=F32))
    flipped = []
    for h in range(PER_STEP):
        out_ref[:, head_cols(h)] = outs[h].astype(BF16)
        flipped.append(outs[h].T.astype(BF16))
    flipped = jnp.concatenate(flipped, axis=0)
    for b in range(GROUP // ROWS):
        block = flipped[b * ROWS : (b + 1) * ROWS]
        out_t_ref[b % NY, b // NY] = jnp.concatenate([block, jnp.zeros((ROWS, PAD - TILE), BF16)], axis=1)


def backward_kernel(
    scalar_ref, q_ref, own_ref, time_ref, core_ref, cross_ref, att_ref, d_ref, probs_ref,
    gq_ref, g_own_ref, g_time_ref, g_core_ref, g_cross_ref,
):
    kv = (own_ref, time_ref, core_ref, cross_ref)
    outs = (g_own_ref, g_time_ref, g_core_ref, g_cross_ref)
    flipped = jnp.concatenate(
        [d_ref[b % NY, b // NY] for b in range(GROUP // ROWS)], axis=0
    )
    d_all = flipped.astype(F32).T[:TILE].astype(BF16)
    ds = [d_all[:, head_cols(h)] for h in range(PER_STEP)]
    d_probs = [
        lax.dot_general(ds[h], window_of(kv, 1, head_cols(h)), NT, preferred_element_type=F32)
        for h in range(PER_STEP)
    ]
    for h in range(PER_STEP):
        value_terms = lax.dot_general(probs_ref[h], ds[h], TN, preferred_element_type=F32)
        for s, ref in enumerate(outs):
            ref[1, :, head_cols(h)] = value_terms[s * TILE : (s + 1) * TILE].astype(ref.dtype)
    for h in range(PER_STEP):
        cols = head_cols(h)
        delta = jnp.sum(ds[h].astype(F32) * att_ref[:, cols].astype(F32), axis=1, keepdims=True)
        d_scores = (probs_ref[h].astype(F32) * (d_probs[h] - delta)).astype(BF16)
        key_terms = lax.dot_general(d_scores, q_ref[:, cols], TN, preferred_element_type=F32) * SCALE
        for s, ref in enumerate(outs):
            ref[0, :, cols] = key_terms[s * TILE : (s + 1) * TILE].astype(ref.dtype)
        gq = jnp.dot(d_scores, window_of(kv, 0, cols), preferred_element_type=F32) * SCALE
        gq_ref[:, cols] = gq.astype(BF16)


def flat_spec(first):
    return pl.BlockSpec((TILE, GROUP), lambda i, b: (0, i + first))


def pair_spec(first):
    return pl.BlockSpec((2, TILE, GROUP), lambda i, b: (0, 0, i + first))


def turned_spec(first):
    return pl.BlockSpec((NY, GROUP // ROWS // NY, ROWS, PAD), lambda i, b: (0, i + first, 0, 0))


def probs_spec(first):
    return pl.BlockSpec((PER_STEP, TILE, SLOTS * TILE), lambda i, b: (i + first, 0, 0))


def whole(shape):
    return pl.BlockSpec(shape, lambda *_: (0,) * len(shape))


def attention_forward(scalars, q, kvs):
    groups = HEADS // PER_STEP
    return pl.pallas_call(
        forward_kernel,
        grid_spec=pltpu.PrefetchScalarGridSpec(
            num_scalar_prefetch=1,
            grid=(groups,),
            in_specs=[flat_spec(0)] + [pair_spec(0)] * 4,
            out_specs=[flat_spec(0), turned_spec(0), probs_spec(0)],
        ),
        out_shape=[
            jax.ShapeDtypeStruct((TILE, groups * GROUP), BF16),
            jax.ShapeDtypeStruct((NY, groups * GROUP // ROWS // NY, ROWS, PAD), BF16),
            jax.ShapeDtypeStruct((HEADS, TILE, SLOTS * TILE), BF16),
        ],
        compiler_params=PARAMS,
        cost_estimate=LIGHT,
    )(scalars, q, *kvs)


def attention_backward(scalars, q, kvs, att, d, probs, first, groups):
    width = groups * GROUP
    return pl.pallas_call(
        backward_kernel,
        grid_spec=pltpu.PrefetchScalarGridSpec(
            num_scalar_prefetch=1,
            grid=(groups,),
            in_specs=[flat_spec(first)] + [pair_spec(first)] * 4 + [flat_spec(first), turned_spec(first), probs_spec(first)],
            out_specs=[flat_spec(0)] + [pair_spec(0)] * 4,
        ),
        out_shape=[jax.ShapeDtypeStruct((TILE, width), BF16)]
        + [jax.ShapeDtypeStruct((2, TILE, width), BF16)] * 4,
        compiler_params=PARAMS,
        cost_estimate=LIGHT,
    )(scalars, q, *kvs, att, d, probs)


def panel_kernel(scalar_ref, weight_ref, after_ref, out_ref):
    for k in range(out_ref.shape[0]):
        out_ref[k] = weight_ref[0]


def panel_copies(scalars, out_weight, copies, after):
    half = out_weight.shape[2] // 2
    return pl.pallas_call(
        panel_kernel,
        grid_spec=pltpu.PrefetchScalarGridSpec(
            num_scalar_prefetch=1,
            grid=(1,),
            in_specs=[
                pl.BlockSpec((1, ROWS, half), lambda i, b: (b[3], 0, b[1])),
                pl.BlockSpec(memory_space=pl.ANY),
            ],
            out_specs=whole((copies, ROWS, half)),
        ),
        out_shape=jax.ShapeDtypeStruct((copies, ROWS, half), BF16),
        compiler_params=PARAMS,
        cost_estimate=LIGHT,
    )(scalars, out_weight, after)


def source(scalar_ref, k):
    return lax.rem(scalar_ref[2] - k + NY, NY)


def d_attention_kernel(scalar_ref, *refs):
    ups, mine_ref, mate_ref, out_ref, weight_ref = refs[:NY], *refs[NY:]
    half = mine_ref.shape[1]
    for side, ref in enumerate((mine_ref, mate_ref)):
        co = scalar_ref[1] if side == 0 else 1 - scalar_ref[1]
        weight_ref[:, pl.ds(pl.multiple_of(co * half, 128), half)] = ref[...]
    for k, up in enumerate(ups):
        out = lax.dot_general(weight_ref[...], up[...], NT, preferred_element_type=F32)
        out_ref[source(scalar_ref, k)] = jnp.concatenate(
            [out.astype(BF16), jnp.zeros((out.shape[0], PAD - TILE), BF16)], axis=1
        )


def d_attention(scalars, ups, w_mine, w_mate):
    dout = ups[0].shape[1]
    rows = w_mine.shape[0]
    return pl.pallas_call(
        d_attention_kernel,
        grid_spec=pltpu.PrefetchScalarGridSpec(
            num_scalar_prefetch=1,
            grid=(1,),
            in_specs=[whole((TILE, dout))] * NY + [whole(w_mine.shape)] * 2,
            out_specs=[whole((NY, rows, PAD)), whole((rows, dout))],
        ),
        out_shape=[
            jax.ShapeDtypeStruct((NY, rows, PAD), BF16),
            jax.ShapeDtypeStruct((rows, dout), BF16),
        ],
        compiler_params=PARAMS,
        cost_estimate=LIGHT,
    )(scalars, *ups, w_mine, w_mate)


def gradient_kernel(scalar_ref, after_ref, att_ref, *refs):
    ups, outs = refs[: 2 * NY], refs[2 * NY :]
    att = jnp.concatenate([att_ref[source(scalar_ref, k)] for k in range(NY)], axis=1)
    rest = jnp.zeros((PAD - TILE, outs[0].shape[1]), BF16)
    for side, out_ref in enumerate(outs):
        up = jnp.concatenate(
            [block for k in range(NY) for block in (ups[side * NY + k][...], rest)], axis=0
        )
        out_ref[...] = jnp.dot(att, up, preferred_element_type=F32).astype(BF16)


def weight_gradient(scalars, atts, ups, after):
    half = ups[0].shape[1] // 2
    rows = atts.shape[1]
    step = 256
    steps = half // step
    mine = pl.BlockSpec((TILE, step), lambda i, b: (0, b[1] * steps + i))
    mate = pl.BlockSpec((TILE, step), lambda i, b: (0, (1 - b[1]) * steps + i))
    return pl.pallas_call(
        gradient_kernel,
        grid_spec=pltpu.PrefetchScalarGridSpec(
            num_scalar_prefetch=1,
            grid=(steps,),
            in_specs=[pl.BlockSpec(memory_space=pl.ANY), whole(atts.shape)] + [mine] * NY + [mate] * NY,
            out_specs=[pl.BlockSpec((rows, step), lambda i, b: (0, i))] * 2,
        ),
        out_shape=[jax.ShapeDtypeStruct((rows, half), BF16)] * 2,
        compiler_params=PARAMS,
        cost_estimate=LIGHT,
    )(scalars, after, atts, *ups, *ups)


def mixed_kernel(scalar_ref, att_ref, weight_ref, *outs):
    for k, out_ref in enumerate(outs):
        att = att_ref[source(scalar_ref, k)][:, :TILE]
        out = lax.dot_general(att, weight_ref[...], TN, preferred_element_type=F32)
        out_ref[...] = out.astype(BF16)


def mixed_parts(scalars, atts, weight):
    rows, dout = weight.shape
    step = 512
    return pl.pallas_call(
        mixed_kernel,
        grid_spec=pltpu.PrefetchScalarGridSpec(
            num_scalar_prefetch=1,
            grid=(dout // step,),
            in_specs=[whole(atts.shape), pl.BlockSpec((rows, step), lambda i, b: (0, i))],
            out_specs=[pl.BlockSpec((TILE, step), lambda i, b: (0, i))] * NY,
        ),
        out_shape=[jax.ShapeDtypeStruct((TILE, dout), BF16)] * NY,
        compiler_params=PARAMS,
        cost_estimate=LIGHT,
    )(scalars, atts, weight)


SWAP = [(0, 1), (1, 0)]
CROSS = [(1, 2), (2, 1)]


def shifted(x, axis, by):
    count = lax.axis_size(axis)
    return lax.ppermute(x, axis, [(i, (i + by) % count) for i in range(count)])


def swapped(x, axis):
    return lax.all_to_all(x, axis, split_axis=0, concat_axis=0, tiled=True)


def per_device(queries, keys_values, upstream, out_weight, block_pick):
    width = queries.shape[4]
    dout = upstream.shape[4]
    half = dout // 2
    rows = out_weight.shape[1]
    ny = lax.axis_size("y")
    nz = lax.axis_size("z")
    co = lax.axis_index("co")
    first = co == 0
    q = queries.reshape(TILE, width)
    kv = keys_values.reshape(2, TILE, width)
    up = upstream.reshape(TILE, dout)

    has_cross = lax.axis_index("xh") != co
    bound = jnp.where(has_cross, SLOTS * TILE, (SLOTS - 1) * TILE)
    scalars = jnp.stack([bound, co, lax.axis_index("y"), block_pick[0]]).astype(jnp.int32)

    from_time = lax.ppermute(kv, "xl", SWAP)
    from_cross = lax.ppermute(kv, ("xh", "co"), CROSS)
    from_core = lax.ppermute(kv, "co", SWAP)

    panels = panel_copies(scalars, out_weight, nz, from_core)
    w_mine = swapped(panels, "z").reshape(nz * rows, half)
    ups = [up] + [shifted(up, "y", k) for k in (1, 2, 3)]
    w_mate = lax.ppermute(w_mine, "co", SWAP)
    d_parts, w_rows = d_attention(scalars, ups, w_mine, w_mate)
    d_turned = swapped(d_parts, "y").reshape(ny, nz, rows, PAD)

    kvs = (kv, from_time, from_core, from_cross)
    kvs, d_parts = lax.optimization_barrier((kvs, d_parts))
    att, att_turned, probs = attention_forward(scalars, q, kvs)
    atts = swapped(att_turned.reshape(ny, nz * rows, PAD), "y")

    parts = 2
    groups = HEADS // PER_STEP // parts

    def backward(c):
        gq, own, to_time, to_core, to_cross = attention_backward(
            scalars, q, kvs, att, d_turned, probs, c * groups, groups
        )
        terms = (
            lax.ppermute(to_time, "xl", SWAP),
            lax.ppermute(to_cross, ("xh", "co"), CROSS),
            lax.ppermute(to_core, "co", SWAP),
        )
        return gq, own, terms

    gq_0, own_0, terms_0 = backward(0)
    grad_mine, grad_mate = weight_gradient(scalars, atts, ups, terms_0[2])
    from_mate = lax.ppermute(grad_mate, "co", SWAP)
    atts, w_rows, grad_mine = lax.optimization_barrier((atts, w_rows, grad_mine))
    mixed = mixed_parts(scalars, atts, w_rows)
    grad = (grad_mine.astype(F32) + from_mate.astype(F32)).astype(BF16).reshape(nz, rows, half)
    probs, grad, mixed = lax.optimization_barrier((probs, grad, mixed))
    gq_1, own_1, terms_1 = backward(1)
    gkv_parts = [
        own.astype(F32) + sum(t.astype(F32) for t in terms)
        for own, terms in ((own_0, terms_0), (own_1, terms_1))
    ]
    gq_parts = (gq_0, gq_1)
    over_z = jnp.sum(swapped(grad, "z").astype(F32), axis=0).astype(BF16)
    x_near = lax.ppermute(over_z, "xl", SWAP)
    x_far = lax.ppermute(over_z, "xh", SWAP)
    x_both = lax.ppermute(over_z, ("xl", "xh"), [(i, 3 - i) for i in range(4)])
    mine = (over_z.astype(F32) + x_near.astype(F32)) + (x_far.astype(F32) + x_both.astype(F32))
    mate = lax.ppermute(mine, "co", SWAP)
    grad_weight = jnp.concatenate(
        [jnp.where(first, mine, mate), jnp.where(first, mate, mine)], axis=1
    )

    back = [shifted(mixed[k], "y", -k).astype(F32) for k in (1, 2, 3)]
    mixed = (mixed[0].astype(F32) + sum(back)).astype(BF16)
    grad_q = jnp.concatenate(gq_parts, axis=1)
    grad_kv = jnp.concatenate([p.astype(BF16) for p in gkv_parts], axis=2)
    return (
        mixed.reshape(upstream.shape),
        grad_q.reshape(queries.shape),
        grad_kv.reshape(keys_values.shape),
        grad_weight,
    )


def solution(mesh):
    fine = Mesh(mesh.devices.reshape(2, 2, 2, 8, 4), ("xl", "xh", "co", "z", "y"))
    wa = ("z", "y")
    ha = ("xh", "co")
    return jax.shard_map(
        per_device,
        mesh=fine,
        in_specs=(
            P(wa, "xl", ha, None, None),
            P(None, wa, "xl", ha, None, None),
            P(wa, "xl", ha, None, None),
            P(None, wa, None),
            P(),
        ),
        out_specs=(
            P(wa, "xl", ha, None, None),
            P(wa, "xl", ha, None, None),
            P(None, wa, "xl", ha, None, None),
            P(wa, None),
        ),
        check_vma=False,
    )
```

```python
import jax
import jax.numpy as jnp
from jax import lax
from jax.experimental import pallas as pl
from jax.experimental.pallas import tpu as pltpu
from jax.sharding import Mesh, PartitionSpec as P

HEADS = 12
HEAD_DIM = 128
SCALE = HEAD_DIM ** (-0.5)
LOG2E = 1.4426950408889634
TILE = 192
SLOTS = 4
PER_STEP = 3
GROUP = PER_STEP * HEAD_DIM
ROWS = 48
NY = 4
PAD = 256
MASKED = 512
NT = (((1,), (1,)), ((), ()))
TN = (((0,), (0,)), ((), ()))
F32 = jnp.float32
BF16 = jnp.bfloat16
LIGHT = pl.CostEstimate(flops=1000, bytes_accessed=1000, transcendentals=0)
PARAMS = pltpu.CompilerParams(vmem_limit_bytes=56 * 1024 * 1024)


def window_of(refs, which, cols):
    return jnp.concatenate([ref[which, :, cols] for ref in refs], axis=0)


def probs_of(scores, bound):
    tail = scores[:, MASKED:]
    column = lax.broadcasted_iota(jnp.int32, tail.shape, 1)
    tail = jnp.where(column + MASKED < bound, tail, -1e30)
    scores = jnp.concatenate([scores[:, :MASKED], tail], axis=1)
    top = jnp.max(scores, axis=1, keepdims=True)
    weights = jnp.exp2((scores - top) * (SCALE * LOG2E))
    return weights * (1.0 / jnp.sum(weights, axis=1, keepdims=True))


def head_cols(h):
    return slice(h * HEAD_DIM, (h + 1) * HEAD_DIM)


def forward_kernel(scalar_ref, q_ref, own_ref, time_ref, core_ref, cross_ref, out_ref, out_t_ref, probs_ref):
    kv = (own_ref, time_ref, core_ref, cross_ref)
    scores = [
        lax.dot_general(
            q_ref[:, head_cols(h)], window_of(kv, 0, head_cols(h)), NT, preferred_element_type=F32
        )
        for h in range(PER_STEP)
    ]
    outs = []
    for h in range(PER_STEP):
        probs_b = probs_of(scores[h], scalar_ref[0]).astype(BF16)
        probs_ref[h] = probs_b
        v = window_of(kv, 1, head_cols(h))
        outs.append(jnp.dot(probs_b, v, preferred_element_type=F32))
    flipped = []
    for h in range(PER_STEP):
        out_ref[:, head_cols(h)] = outs[h].astype(BF16)
        flipped.append(outs[h].T.astype(BF16))
    flipped = jnp.concatenate(flipped, axis=0)
    for b in range(GROUP // ROWS):
        block = flipped[b * ROWS : (b + 1) * ROWS]
        out_t_ref[b % NY, b // NY] = jnp.concatenate([block, jnp.zeros((ROWS, PAD - TILE), BF16)], axis=1)


def backward_kernel(
    scalar_ref, q_ref, own_ref, time_ref, core_ref, cross_ref, att_ref, d_ref, probs_ref,
    gq_ref, g_own_ref, g_time_ref, g_core_ref, g_cross_ref,
):
    kv = (own_ref, time_ref, core_ref, cross_ref)
    outs = (g_own_ref, g_time_ref, g_core_ref, g_cross_ref)
    flipped = jnp.concatenate(
        [d_ref[b % NY, b // NY] for b in range(GROUP // ROWS)], axis=0
    )
    d_all = flipped.astype(F32).T[:TILE].astype(BF16)
    ds = [d_all[:, head_cols(h)] for h in range(PER_STEP)]
    d_probs = [
        lax.dot_general(ds[h], window_of(kv, 1, head_cols(h)), NT, preferred_element_type=F32)
        for h in range(PER_STEP)
    ]
    for h in range(PER_STEP):
        value_terms = lax.dot_general(probs_ref[h], ds[h], TN, preferred_element_type=F32)
        for s, ref in enumerate(outs):
            ref[1, :, head_cols(h)] = value_terms[s * TILE : (s + 1) * TILE].astype(ref.dtype)
    for h in range(PER_STEP):
        cols = head_cols(h)
        delta = jnp.sum(ds[h].astype(F32) * att_ref[:, cols].astype(F32), axis=1, keepdims=True)
        d_scores = (probs_ref[h].astype(F32) * (d_probs[h] - delta)).astype(BF16)
        key_terms = lax.dot_general(d_scores, q_ref[:, cols], TN, preferred_element_type=F32) * SCALE
        for s, ref in enumerate(outs):
            ref[0, :, cols] = key_terms[s * TILE : (s + 1) * TILE].astype(ref.dtype)
        gq = jnp.dot(d_scores, window_of(kv, 0, cols), preferred_element_type=F32) * SCALE
        gq_ref[:, cols] = gq.astype(BF16)


def flat_spec(first):
    return pl.BlockSpec((TILE, GROUP), lambda i, b: (0, i + first))


def pair_spec(first):
    return pl.BlockSpec((2, TILE, GROUP), lambda i, b: (0, 0, i + first))


def turned_spec(first):
    return pl.BlockSpec((NY, GROUP // ROWS // NY, ROWS, PAD), lambda i, b: (0, i + first, 0, 0))


def probs_spec(first):
    return pl.BlockSpec((PER_STEP, TILE, SLOTS * TILE), lambda i, b: (i + first, 0, 0))


def whole(shape):
    return pl.BlockSpec(shape, lambda *_: (0,) * len(shape))


def attention_forward(scalars, q, kvs):
    groups = HEADS // PER_STEP
    return pl.pallas_call(
        forward_kernel,
        grid_spec=pltpu.PrefetchScalarGridSpec(
            num_scalar_prefetch=1,
            grid=(groups,),
            in_specs=[flat_spec(0)] + [pair_spec(0)] * 4,
            out_specs=[flat_spec(0), turned_spec(0), probs_spec(0)],
        ),
        out_shape=[
            jax.ShapeDtypeStruct((TILE, groups * GROUP), BF16),
            jax.ShapeDtypeStruct((NY, groups * GROUP // ROWS // NY, ROWS, PAD), BF16),
            jax.ShapeDtypeStruct((HEADS, TILE, SLOTS * TILE), BF16),
        ],
        compiler_params=PARAMS,
        cost_estimate=LIGHT,
    )(scalars, q, *kvs)


def attention_backward(scalars, q, kvs, att, d, probs, first, groups):
    width = groups * GROUP
    return pl.pallas_call(
        backward_kernel,
        grid_spec=pltpu.PrefetchScalarGridSpec(
            num_scalar_prefetch=1,
            grid=(groups,),
            in_specs=[flat_spec(first)] + [pair_spec(first)] * 4 + [flat_spec(first), turned_spec(first), probs_spec(first)],
            out_specs=[flat_spec(0)] + [pair_spec(0)] * 4,
        ),
        out_shape=[jax.ShapeDtypeStruct((TILE, width), BF16)]
        + [jax.ShapeDtypeStruct((2, TILE, width), BF16)] * 4,
        compiler_params=PARAMS,
        cost_estimate=LIGHT,
    )(scalars, q, *kvs, att, d, probs)


def panel_kernel(scalar_ref, weight_ref, after_ref, out_ref):
    for k in range(out_ref.shape[0]):
        out_ref[k] = weight_ref[0]


def panel_copies(scalars, out_weight, copies, after):
    half = out_weight.shape[2] // 2
    return pl.pallas_call(
        panel_kernel,
        grid_spec=pltpu.PrefetchScalarGridSpec(
            num_scalar_prefetch=1,
            grid=(1,),
            in_specs=[
                pl.BlockSpec((1, ROWS, half), lambda i, b: (b[3], 0, b[1])),
                pl.BlockSpec(memory_space=pl.ANY),
            ],
            out_specs=whole((copies, ROWS, half)),
        ),
        out_shape=jax.ShapeDtypeStruct((copies, ROWS, half), BF16),
        compiler_params=PARAMS,
        cost_estimate=LIGHT,
    )(scalars, out_weight, after)


def source(scalar_ref, k):
    return lax.rem(scalar_ref[2] - k + NY, NY)


def d_attention_kernel(scalar_ref, *refs):
    ups, mine_ref, mate_ref, out_ref, weight_ref = refs[:NY], *refs[NY:]
    half = mine_ref.shape[1]
    for side, ref in enumerate((mine_ref, mate_ref)):
        co = scalar_ref[1] if side == 0 else 1 - scalar_ref[1]
        weight_ref[:, pl.ds(pl.multiple_of(co * half, 128), half)] = ref[...]
    for k, up in enumerate(ups):
        out = lax.dot_general(weight_ref[...], up[...], NT, preferred_element_type=F32)
        out_ref[source(scalar_ref, k)] = jnp.concatenate(
            [out.astype(BF16), jnp.zeros((out.shape[0], PAD - TILE), BF16)], axis=1
        )


def d_attention(scalars, ups, w_mine, w_mate):
    dout = ups[0].shape[1]
    rows = w_mine.shape[0]
    return pl.pallas_call(
        d_attention_kernel,
        grid_spec=pltpu.PrefetchScalarGridSpec(
            num_scalar_prefetch=1,
            grid=(1,),
            in_specs=[whole((TILE, dout))] * NY + [whole(w_mine.shape)] * 2,
            out_specs=[whole((NY, rows, PAD)), whole((rows, dout))],
        ),
        out_shape=[
            jax.ShapeDtypeStruct((NY, rows, PAD), BF16),
            jax.ShapeDtypeStruct((rows, dout), BF16),
        ],
        compiler_params=PARAMS,
        cost_estimate=LIGHT,
    )(scalars, *ups, w_mine, w_mate)


def gradient_kernel(scalar_ref, att_ref, *refs):
    ups, outs = refs[: 2 * NY], refs[2 * NY :]
    att = jnp.concatenate([att_ref[source(scalar_ref, k)] for k in range(NY)], axis=1)
    rest = jnp.zeros((PAD - TILE, outs[0].shape[1]), BF16)
    for side, out_ref in enumerate(outs):
        up = jnp.concatenate(
            [block for k in range(NY) for block in (ups[side * NY + k][...], rest)], axis=0
        )
        out_ref[...] = jnp.dot(att, up, preferred_element_type=F32).astype(BF16)


def weight_gradient(scalars, atts, ups):
    half = ups[0].shape[1] // 2
    rows = atts.shape[1]
    step = 256
    steps = half // step
    mine = pl.BlockSpec((TILE, step), lambda i, b: (0, b[1] * steps + i))
    mate = pl.BlockSpec((TILE, step), lambda i, b: (0, (1 - b[1]) * steps + i))
    return pl.pallas_call(
        gradient_kernel,
        grid_spec=pltpu.PrefetchScalarGridSpec(
            num_scalar_prefetch=1,
            grid=(steps,),
            in_specs=[whole(atts.shape)] + [mine] * NY + [mate] * NY,
            out_specs=[pl.BlockSpec((rows, step), lambda i, b: (0, i))] * 2,
        ),
        out_shape=[jax.ShapeDtypeStruct((rows, half), BF16)] * 2,
        compiler_params=PARAMS,
        cost_estimate=LIGHT,
    )(scalars, atts, *ups, *ups)


def mixed_kernel(scalar_ref, att_ref, weight_ref, *outs):
    for k, out_ref in enumerate(outs):
        att = att_ref[source(scalar_ref, k)][:, :TILE]
        out = lax.dot_general(att, weight_ref[...], TN, preferred_element_type=F32)
        out_ref[...] = out.astype(BF16)


def mixed_parts(scalars, atts, weight):
    rows, dout = weight.shape
    step = 512
    return pl.pallas_call(
        mixed_kernel,
        grid_spec=pltpu.PrefetchScalarGridSpec(
            num_scalar_prefetch=1,
            grid=(dout // step,),
            in_specs=[whole(atts.shape), pl.BlockSpec((rows, step), lambda i, b: (0, i))],
            out_specs=[pl.BlockSpec((TILE, step), lambda i, b: (0, i))] * NY,
        ),
        out_shape=[jax.ShapeDtypeStruct((TILE, dout), BF16)] * NY,
        compiler_params=PARAMS,
        cost_estimate=LIGHT,
    )(scalars, atts, weight)


SWAP = [(0, 1), (1, 0)]
CROSS = [(1, 2), (2, 1)]


def shifted(x, axis, by):
    count = lax.axis_size(axis)
    return lax.ppermute(x, axis, [(i, (i + by) % count) for i in range(count)])


def swapped(x, axis):
    return lax.all_to_all(x, axis, split_axis=0, concat_axis=0, tiled=True)


def per_device(queries, keys_values, upstream, out_weight, block_pick):
    width = queries.shape[4]
    dout = upstream.shape[4]
    half = dout // 2
    rows = out_weight.shape[1]
    ny = lax.axis_size("y")
    nz = lax.axis_size("z")
    co = lax.axis_index("co")
    first = co == 0
    q = queries.reshape(TILE, width)
    kv = keys_values.reshape(2, TILE, width)
    up = upstream.reshape(TILE, dout)

    has_cross = lax.axis_index("xh") != co
    bound = jnp.where(has_cross, SLOTS * TILE, (SLOTS - 1) * TILE)
    scalars = jnp.stack([bound, co, lax.axis_index("y"), block_pick[0]]).astype(jnp.int32)

    from_time = lax.ppermute(kv, "xl", SWAP)
    from_cross = lax.ppermute(kv, ("xh", "co"), CROSS)
    from_core = lax.ppermute(kv, "co", SWAP)

    panels = panel_copies(scalars, out_weight, nz, from_core)
    w_mine = swapped(panels, "z").reshape(nz * rows, half)
    ups = [up] + [shifted(up, "y", k) for k in (1, 2, 3)]
    w_mate = lax.ppermute(w_mine, "co", SWAP)
    d_parts, w_rows = d_attention(scalars, ups, w_mine, w_mate)
    d_turned = swapped(d_parts, "y").reshape(ny, nz, rows, PAD)

    kvs = (kv, from_time, from_core, from_cross)
    att, att_turned, probs = attention_forward(scalars, q, kvs)
    atts = swapped(att_turned.reshape(ny, nz * rows, PAD), "y")

    parts = 2
    groups = HEADS // PER_STEP // parts

    def backward(c):
        gq, own, to_time, to_core, to_cross = attention_backward(
            scalars, q, kvs, att, d_turned, probs, c * groups, groups
        )
        terms = (
            lax.ppermute(to_time, "xl", SWAP),
            lax.ppermute(to_cross, ("xh", "co"), CROSS),
            lax.ppermute(to_core, "co", SWAP),
        )
        return gq, own, terms

    gq_0, own_0, terms_0 = backward(0)
    atts, gq_0 = lax.optimization_barrier((atts, gq_0))
    grad_mine, grad_mate = weight_gradient(scalars, atts, ups)
    from_mate = lax.ppermute(grad_mate, "co", SWAP)
    atts, w_rows, grad_mine = lax.optimization_barrier((atts, w_rows, grad_mine))
    mixed = mixed_parts(scalars, atts, w_rows)
    grad = (grad_mine.astype(F32) + from_mate.astype(F32)).astype(BF16).reshape(nz, rows, half)
    probs, grad, mixed = lax.optimization_barrier((probs, grad, mixed))
    gq_1, own_1, terms_1 = backward(1)
    gkv_parts = [
        own.astype(F32) + sum(t.astype(F32) for t in terms)
        for own, terms in ((own_0, terms_0), (own_1, terms_1))
    ]
    gq_parts = (gq_0, gq_1)
    over_z = jnp.sum(swapped(grad, "z").astype(F32), axis=0).astype(BF16)
    x_near = lax.ppermute(over_z, "xl", SWAP)
    x_far = lax.ppermute(over_z, "xh", SWAP)
    x_both = lax.ppermute(over_z, ("xl", "xh"), [(i, 3 - i) for i in range(4)])
    mine = (over_z.astype(F32) + x_near.astype(F32)) + (x_far.astype(F32) + x_both.astype(F32))
    mate = lax.ppermute(mine, "co", SWAP)
    grad_weight = jnp.concatenate(
        [jnp.where(first, mine, mate), jnp.where(first, mate, mine)], axis=1
    )

    back = [shifted(mixed[k], "y", -k).astype(F32) for k in (1, 2, 3)]
    mixed = (mixed[0].astype(F32) + sum(back)).astype(BF16)
    grad_q = jnp.concatenate(gq_parts, axis=1)
    grad_kv = jnp.concatenate([p.astype(BF16) for p in gkv_parts], axis=2)
    return (
        mixed.reshape(upstream.shape),
        grad_q.reshape(queries.shape),
        grad_kv.reshape(keys_values.shape),
        grad_weight,
    )


def solution(mesh):
    fine = Mesh(mesh.devices.reshape(2, 2, 2, 8, 4), ("xl", "xh", "co", "z", "y"))
    wa = ("z", "y")
    ha = ("xh", "co")
    return jax.shard_map(
        per_device,
        mesh=fine,
        in_specs=(
            P(wa, "xl", ha, None, None),
            P(None, wa, "xl", ha, None, None),
            P(wa, "xl", ha, None, None),
            P(None, wa, None),
            P(),
        ),
        out_specs=(
            P(wa, "xl", ha, None, None),
            P(wa, "xl", ha, None, None),
            P(None, wa, "xl", ha, None, None),
            P(wa, None),
        ),
        check_vma=False,
    )
```

```python
import jax
import jax.numpy as jnp
from jax import lax
from jax.experimental import pallas as pl
from jax.experimental.pallas import tpu as pltpu
from jax.sharding import Mesh, PartitionSpec as P

HEADS = 12
HEAD_DIM = 128
SCALE = HEAD_DIM ** (-0.5)
LOG2E = 1.4426950408889634
TILE = 192
SLOTS = 4
PER_STEP = 3
GROUP = PER_STEP * HEAD_DIM
ROWS = 48
NY = 4
PAD = 256
MASKED = 512
NT = (((1,), (1,)), ((), ()))
TN = (((0,), (0,)), ((), ()))
F32 = jnp.float32
BF16 = jnp.bfloat16
LIGHT = pl.CostEstimate(flops=1000, bytes_accessed=1000, transcendentals=0)
PARAMS = pltpu.CompilerParams(vmem_limit_bytes=56 * 1024 * 1024)


def window_of(refs, which, cols):
    return jnp.concatenate([ref[which, :, cols] for ref in refs], axis=0)


def probs_of(scores, bound):
    tail = scores[:, MASKED:]
    column = lax.broadcasted_iota(jnp.int32, tail.shape, 1)
    tail = jnp.where(column + MASKED < bound, tail, -1e30)
    scores = jnp.concatenate([scores[:, :MASKED], tail], axis=1)
    top = jnp.max(scores, axis=1, keepdims=True)
    weights = jnp.exp2((scores - top) * (SCALE * LOG2E))
    return weights * (1.0 / jnp.sum(weights, axis=1, keepdims=True))


def head_cols(h):
    return slice(h * HEAD_DIM, (h + 1) * HEAD_DIM)


def forward_kernel(scalar_ref, q_ref, own_ref, time_ref, core_ref, cross_ref, out_ref, out_t_ref, probs_ref):
    kv = (own_ref, time_ref, core_ref, cross_ref)
    scores = [
        lax.dot_general(
            q_ref[:, head_cols(h)], window_of(kv, 0, head_cols(h)), NT, preferred_element_type=F32
        )
        for h in range(PER_STEP)
    ]
    outs = []
    for h in range(PER_STEP):
        probs_b = probs_of(scores[h], scalar_ref[0]).astype(BF16)
        probs_ref[h] = probs_b
        v = window_of(kv, 1, head_cols(h))
        outs.append(jnp.dot(probs_b, v, preferred_element_type=F32))
    flipped = []
    for h in range(PER_STEP):
        out_ref[:, head_cols(h)] = outs[h].astype(BF16)
        flipped.append(outs[h].T.astype(BF16))
    flipped = jnp.concatenate(flipped, axis=0)
    for b in range(GROUP // ROWS):
        block = flipped[b * ROWS : (b + 1) * ROWS]
        to = lax.rem(b % NY - scalar_ref[2] + NY, NY)
        out_t_ref[to, b // NY] = jnp.concatenate([block, jnp.zeros((ROWS, PAD - TILE), BF16)], axis=1)


def backward_kernel(
    scalar_ref, q_ref, own_ref, time_ref, core_ref, cross_ref, att_ref, d_ref, probs_ref,
    gq_ref, g_own_ref, g_time_ref, g_core_ref, g_cross_ref,
):
    kv = (own_ref, time_ref, core_ref, cross_ref)
    outs = (g_own_ref, g_time_ref, g_core_ref, g_cross_ref)
    flipped = jnp.concatenate(
        [d_ref[b % NY, b // NY] for b in range(GROUP // ROWS)], axis=0
    )
    d_all = flipped.astype(F32).T[:TILE].astype(BF16)
    ds = [d_all[:, head_cols(h)] for h in range(PER_STEP)]
    d_probs = [
        lax.dot_general(ds[h], window_of(kv, 1, head_cols(h)), NT, preferred_element_type=F32)
        for h in range(PER_STEP)
    ]
    for h in range(PER_STEP):
        value_terms = lax.dot_general(probs_ref[h], ds[h], TN, preferred_element_type=F32)
        for s, ref in enumerate(outs):
            ref[1, :, head_cols(h)] = value_terms[s * TILE : (s + 1) * TILE].astype(ref.dtype)
    for h in range(PER_STEP):
        cols = head_cols(h)
        delta = jnp.sum(ds[h].astype(F32) * att_ref[:, cols].astype(F32), axis=1, keepdims=True)
        d_scores = (probs_ref[h].astype(F32) * (d_probs[h] - delta)).astype(BF16)
        key_terms = lax.dot_general(d_scores, q_ref[:, cols], TN, preferred_element_type=F32) * SCALE
        for s, ref in enumerate(outs):
            ref[0, :, cols] = key_terms[s * TILE : (s + 1) * TILE].astype(ref.dtype)
        gq = jnp.dot(d_scores, window_of(kv, 0, cols), preferred_element_type=F32) * SCALE
        gq_ref[:, cols] = gq.astype(BF16)


def flat_spec(first):
    return pl.BlockSpec((TILE, GROUP), lambda i, b: (0, i + first))


def pair_spec(first):
    return pl.BlockSpec((2, TILE, GROUP), lambda i, b: (0, 0, i + first))


def turned_spec(first):
    return pl.BlockSpec((NY, GROUP // ROWS // NY, ROWS, PAD), lambda i, b: (0, i + first, 0, 0))


def probs_spec(first):
    return pl.BlockSpec((PER_STEP, TILE, SLOTS * TILE), lambda i, b: (i + first, 0, 0))


def whole(shape):
    return pl.BlockSpec(shape, lambda *_: (0,) * len(shape))


def attention_forward(scalars, q, kvs):
    groups = HEADS // PER_STEP
    return pl.pallas_call(
        forward_kernel,
        grid_spec=pltpu.PrefetchScalarGridSpec(
            num_scalar_prefetch=1,
            grid=(groups,),
            in_specs=[flat_spec(0)] + [pair_spec(0)] * 4,
            out_specs=[flat_spec(0), turned_spec(0), probs_spec(0)],
        ),
        out_shape=[
            jax.ShapeDtypeStruct((TILE, groups * GROUP), BF16),
            jax.ShapeDtypeStruct((NY, groups * GROUP // ROWS // NY, ROWS, PAD), BF16),
            jax.ShapeDtypeStruct((HEADS, TILE, SLOTS * TILE), BF16),
        ],
        compiler_params=PARAMS,
        cost_estimate=LIGHT,
    )(scalars, q, *kvs)


def attention_backward(scalars, q, kvs, att, d, probs, first, groups):
    width = groups * GROUP
    return pl.pallas_call(
        backward_kernel,
        grid_spec=pltpu.PrefetchScalarGridSpec(
            num_scalar_prefetch=1,
            grid=(groups,),
            in_specs=[flat_spec(first)] + [pair_spec(first)] * 4 + [flat_spec(first), turned_spec(first), probs_spec(first)],
            out_specs=[flat_spec(0)] + [pair_spec(0)] * 4,
        ),
        out_shape=[jax.ShapeDtypeStruct((TILE, width), BF16)]
        + [jax.ShapeDtypeStruct((2, TILE, width), BF16)] * 4,
        compiler_params=PARAMS,
        cost_estimate=LIGHT,
    )(scalars, q, *kvs, att, d, probs)


def panel_kernel(scalar_ref, weight_ref, out_ref):
    for k in range(out_ref.shape[0]):
        out_ref[k] = weight_ref[0]


def panel_copies(scalars, out_weight, copies):
    half = out_weight.shape[2] // 2
    return pl.pallas_call(
        panel_kernel,
        grid_spec=pltpu.PrefetchScalarGridSpec(
            num_scalar_prefetch=1,
            grid=(1,),
            in_specs=[pl.BlockSpec((1, ROWS, half), lambda i, b: (b[3], 0, b[1]))],
            out_specs=whole((copies, ROWS, half)),
        ),
        out_shape=jax.ShapeDtypeStruct((copies, ROWS, half), BF16),
        compiler_params=PARAMS,
        cost_estimate=LIGHT,
    )(scalars, out_weight)


def source(scalar_ref, k):
    return lax.rem(scalar_ref[2] - k + NY, NY)


def d_attention_kernel(scalar_ref, *refs):
    ups, mine_ref, mate_ref, out_ref, weight_ref = refs[:NY], *refs[NY:]
    half = mine_ref.shape[1]
    for side, ref in enumerate((mine_ref, mate_ref)):
        co = scalar_ref[1] if side == 0 else 1 - scalar_ref[1]
        weight_ref[:, pl.ds(pl.multiple_of(co * half, 128), half)] = ref[...]
    for k, up in enumerate(ups):
        out = lax.dot_general(weight_ref[...], up[...], NT, preferred_element_type=F32)
        out_ref[source(scalar_ref, k)] = jnp.concatenate(
            [out.astype(BF16), jnp.zeros((out.shape[0], PAD - TILE), BF16)], axis=1
        )


def d_attention(scalars, ups, w_mine, w_mate):
    dout = ups[0].shape[1]
    rows = w_mine.shape[0]
    return pl.pallas_call(
        d_attention_kernel,
        grid_spec=pltpu.PrefetchScalarGridSpec(
            num_scalar_prefetch=1,
            grid=(1,),
            in_specs=[whole((TILE, dout))] * NY + [whole(w_mine.shape)] * 2,
            out_specs=[whole((NY, rows, PAD)), whole((rows, dout))],
        ),
        out_shape=[
            jax.ShapeDtypeStruct((NY, rows, PAD), BF16),
            jax.ShapeDtypeStruct((rows, dout), BF16),
        ],
        compiler_params=PARAMS,
        cost_estimate=LIGHT,
    )(scalars, *ups, w_mine, w_mate)


def gradient_kernel(scalar_ref, *refs):
    atts, ups, outs = refs[:NY], refs[NY : 3 * NY], refs[3 * NY :]
    att = jnp.concatenate([ref[...] for ref in atts], axis=1)
    rest = jnp.zeros((PAD - TILE, outs[0].shape[1]), BF16)
    for side, out_ref in enumerate(outs):
        up = jnp.concatenate(
            [block for k in range(NY) for block in (ups[side * NY + k][...], rest)], axis=0
        )
        out_ref[...] = jnp.dot(att, up, preferred_element_type=F32).astype(BF16)


def weight_gradient(scalars, atts, ups):
    half = ups[0].shape[1] // 2
    rows = atts[0].shape[0]
    step = 256
    steps = half // step
    mine = pl.BlockSpec((TILE, step), lambda i, b: (0, b[1] * steps + i))
    mate = pl.BlockSpec((TILE, step), lambda i, b: (0, (1 - b[1]) * steps + i))
    return pl.pallas_call(
        gradient_kernel,
        grid_spec=pltpu.PrefetchScalarGridSpec(
            num_scalar_prefetch=1,
            grid=(steps,),
            in_specs=[whole((rows, PAD))] * NY + [mine] * NY + [mate] * NY,
            out_specs=[pl.BlockSpec((rows, step), lambda i, b: (0, i))] * 2,
        ),
        out_shape=[jax.ShapeDtypeStruct((rows, half), BF16)] * 2,
        compiler_params=PARAMS,
        cost_estimate=LIGHT,
    )(scalars, *atts, *ups, *ups)


def mixed_kernel(*refs):
    atts, weight_ref, outs = refs[:NY], refs[NY], refs[NY + 1 :]
    for att_ref, out_ref in zip(atts, outs):
        att = att_ref[...][:, :TILE]
        out = lax.dot_general(att, weight_ref[...], TN, preferred_element_type=F32)
        out_ref[...] = out.astype(BF16)


def mixed_parts(atts, weight):
    rows, dout = weight.shape
    step = 512
    return pl.pallas_call(
        mixed_kernel,
        grid=(dout // step,),
        in_specs=[whole((rows, PAD))] * NY + [pl.BlockSpec((rows, step), lambda i: (0, i))],
        out_specs=[pl.BlockSpec((TILE, step), lambda i: (0, i))] * NY,
        out_shape=[jax.ShapeDtypeStruct((TILE, dout), BF16)] * NY,
        compiler_params=PARAMS,
        cost_estimate=LIGHT,
    )(*atts, weight)


SWAP = [(0, 1), (1, 0)]
CROSS = [(1, 2), (2, 1)]


def shifted(x, axis, by):
    count = lax.axis_size(axis)
    return lax.ppermute(x, axis, [(i, (i + by) % count) for i in range(count)])


def swapped(x, axis):
    return lax.all_to_all(x, axis, split_axis=0, concat_axis=0, tiled=True)


def per_device(queries, keys_values, upstream, out_weight, block_pick):
    width = queries.shape[4]
    dout = upstream.shape[4]
    half = dout // 2
    rows = out_weight.shape[1]
    ny = lax.axis_size("y")
    nz = lax.axis_size("z")
    co = lax.axis_index("co")
    first = co == 0
    q = queries.reshape(TILE, width)
    kv = keys_values.reshape(2, TILE, width)
    up = upstream.reshape(TILE, dout)

    has_cross = lax.axis_index("xh") != co
    bound = jnp.where(has_cross, SLOTS * TILE, (SLOTS - 1) * TILE)
    scalars = jnp.stack([bound, co, lax.axis_index("y"), block_pick[0]]).astype(jnp.int32)

    from_time = lax.ppermute(kv, "xl", SWAP)
    from_cross = lax.ppermute(kv, ("xh", "co"), CROSS)
    from_core = lax.ppermute(kv, "co", SWAP)

    panels = panel_copies(scalars, out_weight, nz)
    w_mine = swapped(panels, "z").reshape(nz * rows, half)
    ups = [up] + [shifted(up, "y", k) for k in (1, 2, 3)]
    w_mate = lax.ppermute(w_mine, "co", SWAP)
    kvs = (kv, from_time, from_core, from_cross)
    att, att_turned, probs = attention_forward(scalars, q, kvs)
    att_turned = att_turned.reshape(ny, nz * rows, PAD)
    atts = [att_turned[0]] + [shifted(att_turned[k], "y", k) for k in (1, 2, 3)]
    att, w_mine, w_mate = lax.optimization_barrier((att, w_mine, w_mate))
    d_parts, w_rows = d_attention(scalars, ups, w_mine, w_mate)
    d_turned = swapped(d_parts, "y").reshape(ny, nz, rows, PAD)

    parts = 2
    groups = HEADS // PER_STEP // parts

    def backward(c):
        gq, own, to_time, to_core, to_cross = attention_backward(
            scalars, q, kvs, att, d_turned, probs, c * groups, groups
        )
        terms = (
            lax.ppermute(to_time, "xl", SWAP),
            lax.ppermute(to_cross, ("xh", "co"), CROSS),
            lax.ppermute(to_core, "co", SWAP),
        )
        return gq, own, terms

    gq_0, own_0, terms_0 = backward(0)
    atts, gq_0 = lax.optimization_barrier((atts, gq_0))
    grad_mine, grad_mate = weight_gradient(scalars, atts, ups)
    from_mate = lax.ppermute(grad_mate, "co", SWAP)
    atts, w_rows, grad_mine = lax.optimization_barrier((atts, w_rows, grad_mine))
    mixed = mixed_parts(atts, w_rows)
    grad = (grad_mine.astype(F32) + from_mate.astype(F32)).astype(BF16).reshape(nz, rows, half)
    probs, grad, mixed = lax.optimization_barrier((probs, grad, mixed))
    gq_1, own_1, terms_1 = backward(1)
    gkv_parts = [
        own.astype(F32) + sum(t.astype(F32) for t in terms)
        for own, terms in ((own_0, terms_0), (own_1, terms_1))
    ]
    gq_parts = (gq_0, gq_1)
    over_z = jnp.sum(swapped(grad, "z").astype(F32), axis=0).astype(BF16)
    x_near = lax.ppermute(over_z, "xl", SWAP)
    x_far = lax.ppermute(over_z, "xh", SWAP)
    x_both = lax.ppermute(over_z, ("xl", "xh"), [(i, 3 - i) for i in range(4)])
    mine = (over_z.astype(F32) + x_near.astype(F32)) + (x_far.astype(F32) + x_both.astype(F32))
    mate = lax.ppermute(mine, "co", SWAP)
    grad_weight = jnp.concatenate(
        [jnp.where(first, mine, mate), jnp.where(first, mate, mine)], axis=1
    )

    back = [shifted(mixed[k], "y", -k).astype(F32) for k in (1, 2, 3)]
    mixed = (mixed[0].astype(F32) + sum(back)).astype(BF16)
    grad_q = jnp.concatenate(gq_parts, axis=1)
    grad_kv = jnp.concatenate([p.astype(BF16) for p in gkv_parts], axis=2)
    return (
        mixed.reshape(upstream.shape),
        grad_q.reshape(queries.shape),
        grad_kv.reshape(keys_values.shape),
        grad_weight,
    )


def solution(mesh):
    fine = Mesh(mesh.devices.reshape(2, 2, 2, 8, 4), ("xl", "xh", "co", "z", "y"))
    wa = ("z", "y")
    ha = ("xh", "co")
    return jax.shard_map(
        per_device,
        mesh=fine,
        in_specs=(
            P(wa, "xl", ha, None, None),
            P(None, wa, "xl", ha, None, None),
            P(wa, "xl", ha, None, None),
            P(None, wa, None),
            P(),
        ),
        out_specs=(
            P(wa, "xl", ha, None, None),
            P(wa, "xl", ha, None, None),
            P(None, wa, "xl", ha, None, None),
            P(wa, None),
        ),
        check_vma=False,
    )
```

```python
import jax
import jax.numpy as jnp
from jax import lax
from jax.experimental import pallas as pl
from jax.experimental.pallas import tpu as pltpu
from jax.sharding import Mesh, PartitionSpec as P

HEADS = 12
HEAD_DIM = 128
SCALE = HEAD_DIM ** (-0.5)
LOG2E = 1.4426950408889634
TILE = 192
SLOTS = 4
PER_STEP = 3
GROUP = PER_STEP * HEAD_DIM
ROWS = 48
NY = 4
PAD = 256
MASKED = 512
NT = (((1,), (1,)), ((), ()))
TN = (((0,), (0,)), ((), ()))
F32 = jnp.float32
BF16 = jnp.bfloat16
LIGHT = pl.CostEstimate(flops=1000, bytes_accessed=1000, transcendentals=0)
PARAMS = pltpu.CompilerParams(vmem_limit_bytes=56 * 1024 * 1024)


def window_of(refs, which, cols):
    return jnp.concatenate([ref[which, :, cols] for ref in refs], axis=0)


def probs_of(scores, bound):
    tail = scores[:, MASKED:]
    column = lax.broadcasted_iota(jnp.int32, tail.shape, 1)
    tail = jnp.where(column + MASKED < bound, tail, -1e30)
    scores = jnp.concatenate([scores[:, :MASKED], tail], axis=1)
    top = jnp.max(scores, axis=1, keepdims=True)
    weights = jnp.exp2((scores - top) * (SCALE * LOG2E))
    return weights * (1.0 / jnp.sum(weights, axis=1, keepdims=True))


def head_cols(h):
    return slice(h * HEAD_DIM, (h + 1) * HEAD_DIM)


def forward_kernel(scalar_ref, q_ref, own_ref, time_ref, core_ref, cross_ref, out_ref, out_t_ref, probs_ref):
    kv = (own_ref, time_ref, core_ref, cross_ref)
    scores = [
        lax.dot_general(
            q_ref[:, head_cols(h)], window_of(kv, 0, head_cols(h)), NT, preferred_element_type=F32
        )
        for h in range(PER_STEP)
    ]
    outs = []
    for h in range(PER_STEP):
        probs_b = probs_of(scores[h], scalar_ref[0]).astype(BF16)
        probs_ref[h] = probs_b
        v = window_of(kv, 1, head_cols(h))
        outs.append(jnp.dot(probs_b, v, preferred_element_type=F32))
    flipped = []
    for h in range(PER_STEP):
        out_ref[:, head_cols(h)] = outs[h].astype(BF16)
        flipped.append(outs[h].T.astype(BF16))
    flipped = jnp.concatenate(flipped, axis=0)
    for b in range(GROUP // ROWS):
        block = flipped[b * ROWS : (b + 1) * ROWS]
        out_t_ref[b % NY, b // NY] = jnp.concatenate([block, jnp.zeros((ROWS, PAD - TILE), BF16)], axis=1)


def backward_kernel(
    scalar_ref, q_ref, own_ref, time_ref, core_ref, cross_ref, att_ref, d_ref, probs_ref,
    gq_ref, g_own_ref, g_time_ref, g_core_ref, g_cross_ref,
):
    kv = (own_ref, time_ref, core_ref, cross_ref)
    outs = (g_own_ref, g_time_ref, g_core_ref, g_cross_ref)
    flipped = jnp.concatenate(
        [d_ref[b % NY, b // NY] for b in range(GROUP // ROWS)], axis=0
    )
    d_all = flipped.astype(F32).T[:TILE].astype(BF16)
    ds = [d_all[:, head_cols(h)] for h in range(PER_STEP)]
    d_probs = [
        lax.dot_general(ds[h], window_of(kv, 1, head_cols(h)), NT, preferred_element_type=F32)
        for h in range(PER_STEP)
    ]
    for h in range(PER_STEP):
        value_terms = lax.dot_general(probs_ref[h], ds[h], TN, preferred_element_type=F32)
        for s, ref in enumerate(outs):
            ref[1, :, head_cols(h)] = value_terms[s * TILE : (s + 1) * TILE].astype(ref.dtype)
    for h in range(PER_STEP):
        cols = head_cols(h)
        delta = jnp.sum(ds[h].astype(F32) * att_ref[:, cols].astype(F32), axis=1, keepdims=True)
        d_scores = (probs_ref[h].astype(F32) * (d_probs[h] - delta)).astype(BF16)
        key_terms = lax.dot_general(d_scores, q_ref[:, cols], TN, preferred_element_type=F32) * SCALE
        for s, ref in enumerate(outs):
            ref[0, :, cols] = key_terms[s * TILE : (s + 1) * TILE].astype(ref.dtype)
        gq = jnp.dot(d_scores, window_of(kv, 0, cols), preferred_element_type=F32) * SCALE
        gq_ref[:, cols] = gq.astype(BF16)


def flat_spec(first):
    return pl.BlockSpec((TILE, GROUP), lambda i, b: (0, i + first))


def pair_spec(first):
    return pl.BlockSpec((2, TILE, GROUP), lambda i, b: (0, 0, i + first))


def turned_spec(first):
    return pl.BlockSpec((NY, GROUP // ROWS // NY, ROWS, PAD), lambda i, b: (0, i + first, 0, 0))


def probs_spec(first):
    return pl.BlockSpec((PER_STEP, TILE, SLOTS * TILE), lambda i, b: (i + first, 0, 0))


def whole(shape):
    return pl.BlockSpec(shape, lambda *_: (0,) * len(shape))


def attention_forward(scalars, q, kvs):
    groups = HEADS // PER_STEP
    return pl.pallas_call(
        forward_kernel,
        grid_spec=pltpu.PrefetchScalarGridSpec(
            num_scalar_prefetch=1,
            grid=(groups,),
            in_specs=[flat_spec(0)] + [pair_spec(0)] * 4,
            out_specs=[flat_spec(0), turned_spec(0), probs_spec(0)],
        ),
        out_shape=[
            jax.ShapeDtypeStruct((TILE, groups * GROUP), BF16),
            jax.ShapeDtypeStruct((NY, groups * GROUP // ROWS // NY, ROWS, PAD), BF16),
            jax.ShapeDtypeStruct((HEADS, TILE, SLOTS * TILE), BF16),
        ],
        compiler_params=PARAMS,
        cost_estimate=LIGHT,
    )(scalars, q, *kvs)


def attention_backward(scalars, q, kvs, att, d, probs, first, groups):
    width = groups * GROUP
    return pl.pallas_call(
        backward_kernel,
        grid_spec=pltpu.PrefetchScalarGridSpec(
            num_scalar_prefetch=1,
            grid=(groups,),
            in_specs=[flat_spec(first)] + [pair_spec(first)] * 4 + [flat_spec(first), turned_spec(first), probs_spec(first)],
            out_specs=[flat_spec(0)] + [pair_spec(0)] * 4,
        ),
        out_shape=[jax.ShapeDtypeStruct((TILE, width), BF16)]
        + [jax.ShapeDtypeStruct((2, TILE, width), BF16)] * 4,
        compiler_params=PARAMS,
        cost_estimate=LIGHT,
    )(scalars, q, *kvs, att, d, probs)


def panel_kernel(scalar_ref, weight_ref, out_ref):
    for k in range(out_ref.shape[0]):
        out_ref[k] = weight_ref[0]


def panel_copies(scalars, out_weight, copies):
    half = out_weight.shape[2] // 2
    return pl.pallas_call(
        panel_kernel,
        grid_spec=pltpu.PrefetchScalarGridSpec(
            num_scalar_prefetch=1,
            grid=(1,),
            in_specs=[pl.BlockSpec((1, ROWS, half), lambda i, b: (b[3], 0, b[1]))],
            out_specs=whole((copies, ROWS, half)),
        ),
        out_shape=jax.ShapeDtypeStruct((copies, ROWS, half), BF16),
        compiler_params=PARAMS,
        cost_estimate=LIGHT,
    )(scalars, out_weight)


def source(scalar_ref, k):
    return lax.rem(scalar_ref[2] - k + NY, NY)


def d_attention_kernel(scalar_ref, *refs):
    ups, mine_ref, mate_ref, out_ref, weight_ref = refs[:NY], *refs[NY:]
    half = mine_ref.shape[1]
    for side, ref in enumerate((mine_ref, mate_ref)):
        co = scalar_ref[1] if side == 0 else 1 - scalar_ref[1]
        weight_ref[:, pl.ds(pl.multiple_of(co * half, 128), half)] = ref[...]
    for k, up in enumerate(ups):
        out = lax.dot_general(weight_ref[...], up[...], NT, preferred_element_type=F32)
        out_ref[source(scalar_ref, k)] = jnp.concatenate(
            [out.astype(BF16), jnp.zeros((out.shape[0], PAD - TILE), BF16)], axis=1
        )


def d_attention(scalars, ups, w_mine, w_mate):
    dout = ups[0].shape[1]
    rows = w_mine.shape[0]
    return pl.pallas_call(
        d_attention_kernel,
        grid_spec=pltpu.PrefetchScalarGridSpec(
            num_scalar_prefetch=1,
            grid=(1,),
            in_specs=[whole((TILE, dout))] * NY + [whole(w_mine.shape)] * 2,
            out_specs=[whole((NY, rows, PAD)), whole((rows, dout))],
        ),
        out_shape=[
            jax.ShapeDtypeStruct((NY, rows, PAD), BF16),
            jax.ShapeDtypeStruct((rows, dout), BF16),
        ],
        compiler_params=PARAMS,
        cost_estimate=LIGHT,
    )(scalars, *ups, w_mine, w_mate)


def gradient_kernel(scalar_ref, att_ref, *refs):
    ups, outs = refs[: 2 * NY], refs[2 * NY :]
    att = jnp.concatenate([att_ref[source(scalar_ref, k)] for k in range(NY)], axis=1)
    rest = jnp.zeros((PAD - TILE, outs[0].shape[1]), BF16)
    for side, out_ref in enumerate(outs):
        up = jnp.concatenate(
            [block for k in range(NY) for block in (ups[side * NY + k][...], rest)], axis=0
        )
        out_ref[...] = jnp.dot(att, up, preferred_element_type=F32).astype(BF16)


def weight_gradient(scalars, atts, ups):
    half = ups[0].shape[1] // 2
    rows = atts.shape[1]
    step = 256
    steps = half // step
    mine = pl.BlockSpec((TILE, step), lambda i, b: (0, b[1] * steps + i))
    mate = pl.BlockSpec((TILE, step), lambda i, b: (0, (1 - b[1]) * steps + i))
    return pl.pallas_call(
        gradient_kernel,
        grid_spec=pltpu.PrefetchScalarGridSpec(
            num_scalar_prefetch=1,
            grid=(steps,),
            in_specs=[whole(atts.shape)] + [mine] * NY + [mate] * NY,
            out_specs=[pl.BlockSpec((rows, step), lambda i, b: (0, i))] * 2,
        ),
        out_shape=[jax.ShapeDtypeStruct((rows, half), BF16)] * 2,
        compiler_params=PARAMS,
        cost_estimate=LIGHT,
    )(scalars, atts, *ups, *ups)


def mixed_kernel(scalar_ref, att_ref, weight_ref, *outs):
    for k, out_ref in enumerate(outs):
        att = att_ref[source(scalar_ref, k)][:, :TILE]
        out = lax.dot_general(att, weight_ref[...], TN, preferred_element_type=F32)
        out_ref[...] = out.astype(BF16)


def mixed_parts(scalars, atts, weight):
    rows, dout = weight.shape
    step = 512
    return pl.pallas_call(
        mixed_kernel,
        grid_spec=pltpu.PrefetchScalarGridSpec(
            num_scalar_prefetch=1,
            grid=(dout // step,),
            in_specs=[whole(atts.shape), pl.BlockSpec((rows, step), lambda i, b: (0, i))],
            out_specs=[pl.BlockSpec((TILE, step), lambda i, b: (0, i))] * NY,
        ),
        out_shape=[jax.ShapeDtypeStruct((TILE, dout), BF16)] * NY,
        compiler_params=PARAMS,
        cost_estimate=LIGHT,
    )(scalars, atts, weight)


SWAP = [(0, 1), (1, 0)]
CROSS = [(1, 2), (2, 1)]


def shifted(x, axis, by):
    count = lax.axis_size(axis)
    return lax.ppermute(x, axis, [(i, (i + by) % count) for i in range(count)])


def swapped(x, axis):
    return lax.all_to_all(x, axis, split_axis=0, concat_axis=0, tiled=True)


def per_device(queries, keys_values, upstream, out_weight, block_pick):
    width = queries.shape[4]
    dout = upstream.shape[4]
    half = dout // 2
    rows = out_weight.shape[1]
    ny = lax.axis_size("y")
    nz = lax.axis_size("z")
    co = lax.axis_index("co")
    first = co == 0
    q = queries.reshape(TILE, width)
    kv = keys_values.reshape(2, TILE, width)
    up = upstream.reshape(TILE, dout)

    has_cross = lax.axis_index("xh") != co
    bound = jnp.where(has_cross, SLOTS * TILE, (SLOTS - 1) * TILE)
    scalars = jnp.stack([bound, co, lax.axis_index("y"), block_pick[0]]).astype(jnp.int32)

    from_time = lax.ppermute(kv, "xl", SWAP)
    from_cross = lax.ppermute(kv, ("xh", "co"), CROSS)
    from_core = lax.ppermute(kv, "co", SWAP)

    panels = panel_copies(scalars, out_weight, nz)
    w_mine = swapped(panels, "z").reshape(nz * rows, half)
    ups = [up] + [shifted(up, "y", k) for k in (1, 2, 3)]
    w_mate = lax.ppermute(w_mine, "co", SWAP)
    d_parts, w_rows = d_attention(scalars, ups, w_mine, w_mate)
    d_turned = swapped(d_parts, "y").reshape(ny, nz, rows, PAD)

    kvs = (kv, from_time, from_core, from_cross)
    att, att_turned, probs = attention_forward(scalars, q, kvs)
    atts = swapped(att_turned.reshape(ny, nz * rows, PAD), "y")

    parts = 2
    groups = HEADS // PER_STEP // parts

    def backward(c):
        gq, own, to_time, to_core, to_cross = attention_backward(
            scalars, q, kvs, att, d_turned, probs, c * groups, groups
        )
        terms = (
            lax.ppermute(to_time, "xl", SWAP),
            lax.ppermute(to_cross, ("xh", "co"), CROSS),
            lax.ppermute(to_core, "co", SWAP),
        )
        return gq, own, terms

    gq_0, own_0, terms_0 = backward(0)
    gq_1, own_1, terms_1 = backward(1)
    atts, gq_0, gq_1 = lax.optimization_barrier((atts, gq_0, gq_1))
    grad_mine, grad_mate = weight_gradient(scalars, atts, ups)
    from_mate = lax.ppermute(grad_mate, "co", SWAP)
    grad = (grad_mine.astype(F32) + from_mate.astype(F32)).astype(BF16).reshape(nz, rows, half)
    atts, w_rows, grad = lax.optimization_barrier((atts, w_rows, grad))
    mixed = mixed_parts(scalars, atts, w_rows)
    gkv_parts = [
        own.astype(F32) + sum(t.astype(F32) for t in terms)
        for own, terms in ((own_0, terms_0), (own_1, terms_1))
    ]
    gq_parts = (gq_0, gq_1)
    over_z = jnp.sum(swapped(grad, "z").astype(F32), axis=0).astype(BF16)
    x_near = lax.ppermute(over_z, "xl", SWAP)
    x_far = lax.ppermute(over_z, "xh", SWAP)
    x_both = lax.ppermute(over_z, ("xl", "xh"), [(i, 3 - i) for i in range(4)])
    mine = (over_z.astype(F32) + x_near.astype(F32)) + (x_far.astype(F32) + x_both.astype(F32))
    mate = lax.ppermute(mine, "co", SWAP)
    grad_weight = jnp.concatenate(
        [jnp.where(first, mine, mate), jnp.where(first, mate, mine)], axis=1
    )

    back = [shifted(mixed[k], "y", -k).astype(F32) for k in (1, 2, 3)]
    mixed = (mixed[0].astype(F32) + sum(back)).astype(BF16)
    grad_q = jnp.concatenate(gq_parts, axis=1)
    grad_kv = jnp.concatenate([p.astype(BF16) for p in gkv_parts], axis=2)
    return (
        mixed.reshape(upstream.shape),
        grad_q.reshape(queries.shape),
        grad_kv.reshape(keys_values.shape),
        grad_weight,
    )


def solution(mesh):
    fine = Mesh(mesh.devices.reshape(2, 2, 2, 8, 4), ("xl", "xh", "co", "z", "y"))
    wa = ("z", "y")
    ha = ("xh", "co")
    return jax.shard_map(
        per_device,
        mesh=fine,
        in_specs=(
            P(wa, "xl", ha, None, None),
            P(None, wa, "xl", ha, None, None),
            P(wa, "xl", ha, None, None),
            P(None, wa, None),
            P(),
        ),
        out_specs=(
            P(wa, "xl", ha, None, None),
            P(wa, "xl", ha, None, None),
            P(None, wa, "xl", ha, None, None),
            P(wa, None),
        ),
        check_vma=False,
    )
```

```python
import jax
import jax.numpy as jnp
from jax import lax
from jax.experimental import pallas as pl
from jax.experimental.pallas import tpu as pltpu
from jax.sharding import Mesh, PartitionSpec as P

HEADS = 12
HEAD_DIM = 128
SCALE = HEAD_DIM ** (-0.5)
LOG2E = 1.4426950408889634
TILE = 192
SLOTS = 4
PER_STEP = 3
GROUP = PER_STEP * HEAD_DIM
ROWS = 48
NY = 4
PAD = 256
MASKED = 512
NT = (((1,), (1,)), ((), ()))
TN = (((0,), (0,)), ((), ()))
F32 = jnp.float32
BF16 = jnp.bfloat16
LIGHT = pl.CostEstimate(flops=1000, bytes_accessed=1000, transcendentals=0)
PARAMS = pltpu.CompilerParams(vmem_limit_bytes=56 * 1024 * 1024)


def window_of(refs, which, cols):
    return jnp.concatenate([ref[which, :, cols] for ref in refs], axis=0)


def probs_of(scores, bound):
    tail = scores[:, MASKED:]
    column = lax.broadcasted_iota(jnp.int32, tail.shape, 1)
    tail = jnp.where(column + MASKED < bound, tail, -1e30)
    scores = jnp.concatenate([scores[:, :MASKED], tail], axis=1)
    top = jnp.max(scores, axis=1, keepdims=True)
    weights = jnp.exp2((scores - top) * (SCALE * LOG2E))
    return weights * (1.0 / jnp.sum(weights, axis=1, keepdims=True))


def head_cols(h):
    return slice(h * HEAD_DIM, (h + 1) * HEAD_DIM)


def forward_kernel(scalar_ref, q_ref, own_ref, time_ref, core_ref, cross_ref, out_ref, out_t_ref, probs_ref):
    kv = (own_ref, time_ref, core_ref, cross_ref)
    scores = [
        lax.dot_general(
            q_ref[:, head_cols(h)], window_of(kv, 0, head_cols(h)), NT, preferred_element_type=F32
        )
        for h in range(PER_STEP)
    ]
    outs = []
    for h in range(PER_STEP):
        probs_b = probs_of(scores[h], scalar_ref[0]).astype(BF16)
        probs_ref[h] = probs_b
        v = window_of(kv, 1, head_cols(h))
        outs.append(jnp.dot(probs_b, v, preferred_element_type=F32))
    flipped = []
    for h in range(PER_STEP):
        out_ref[:, head_cols(h)] = outs[h].astype(BF16)
        flipped.append(outs[h].T.astype(BF16))
    flipped = jnp.concatenate(flipped, axis=0)
    for b in range(GROUP // ROWS):
        block = flipped[b * ROWS : (b + 1) * ROWS]
        out_t_ref[b % NY, b // NY] = jnp.concatenate([block, jnp.zeros((ROWS, PAD - TILE), BF16)], axis=1)


def backward_kernel(
    scalar_ref, q_ref, own_ref, time_ref, core_ref, cross_ref, att_ref, d_ref, probs_ref,
    gq_ref, g_own_ref, g_time_ref, g_core_ref, g_cross_ref,
):
    kv = (own_ref, time_ref, core_ref, cross_ref)
    outs = (g_own_ref, g_time_ref, g_core_ref, g_cross_ref)
    flipped = jnp.concatenate(
        [d_ref[b % NY, b // NY] for b in range(GROUP // ROWS)], axis=0
    )
    d_all = flipped.astype(F32).T[:TILE].astype(BF16)
    ds = [d_all[:, head_cols(h)] for h in range(PER_STEP)]
    d_probs = [
        lax.dot_general(ds[h], window_of(kv, 1, head_cols(h)), NT, preferred_element_type=F32)
        for h in range(PER_STEP)
    ]
    for h in range(PER_STEP):
        value_terms = lax.dot_general(probs_ref[h], ds[h], TN, preferred_element_type=F32)
        for s, ref in enumerate(outs):
            ref[1, :, head_cols(h)] = value_terms[s * TILE : (s + 1) * TILE].astype(ref.dtype)
    for h in range(PER_STEP):
        cols = head_cols(h)
        delta = jnp.sum(ds[h].astype(F32) * att_ref[:, cols].astype(F32), axis=1, keepdims=True)
        d_scores = (probs_ref[h].astype(F32) * (d_probs[h] - delta)).astype(BF16)
        key_terms = lax.dot_general(d_scores, q_ref[:, cols], TN, preferred_element_type=F32) * SCALE
        for s, ref in enumerate(outs):
            ref[0, :, cols] = key_terms[s * TILE : (s + 1) * TILE].astype(ref.dtype)
        gq = jnp.dot(d_scores, window_of(kv, 0, cols), preferred_element_type=F32) * SCALE
        gq_ref[:, cols] = gq.astype(BF16)


def flat_spec(first):
    return pl.BlockSpec((TILE, GROUP), lambda i, b: (0, i + first))


def pair_spec(first):
    return pl.BlockSpec((2, TILE, GROUP), lambda i, b: (0, 0, i + first))


def turned_spec(first):
    return pl.BlockSpec((NY, GROUP // ROWS // NY, ROWS, PAD), lambda i, b: (0, i + first, 0, 0))


def probs_spec(first):
    return pl.BlockSpec((PER_STEP, TILE, SLOTS * TILE), lambda i, b: (i + first, 0, 0))


def whole(shape):
    return pl.BlockSpec(shape, lambda *_: (0,) * len(shape))


def attention_forward(scalars, q, kvs):
    groups = HEADS // PER_STEP
    return pl.pallas_call(
        forward_kernel,
        grid_spec=pltpu.PrefetchScalarGridSpec(
            num_scalar_prefetch=1,
            grid=(groups,),
            in_specs=[flat_spec(0)] + [pair_spec(0)] * 4,
            out_specs=[flat_spec(0), turned_spec(0), probs_spec(0)],
        ),
        out_shape=[
            jax.ShapeDtypeStruct((TILE, groups * GROUP), BF16),
            jax.ShapeDtypeStruct((NY, groups * GROUP // ROWS // NY, ROWS, PAD), BF16),
            jax.ShapeDtypeStruct((HEADS, TILE, SLOTS * TILE), BF16),
        ],
        compiler_params=PARAMS,
        cost_estimate=LIGHT,
    )(scalars, q, *kvs)


def attention_backward(scalars, q, kvs, att, d, probs, first, groups):
    width = groups * GROUP
    return pl.pallas_call(
        backward_kernel,
        grid_spec=pltpu.PrefetchScalarGridSpec(
            num_scalar_prefetch=1,
            grid=(groups,),
            in_specs=[flat_spec(first)] + [pair_spec(first)] * 4 + [flat_spec(first), turned_spec(first), probs_spec(first)],
            out_specs=[flat_spec(0)] + [pair_spec(0)] * 4,
        ),
        out_shape=[jax.ShapeDtypeStruct((TILE, width), BF16)]
        + [jax.ShapeDtypeStruct((2, TILE, width), BF16)] * 4,
        compiler_params=PARAMS,
        cost_estimate=LIGHT,
    )(scalars, q, *kvs, att, d, probs)


def panel_kernel(scalar_ref, weight_ref, out_ref):
    for k in range(out_ref.shape[0]):
        out_ref[k] = weight_ref[0]


def panel_copies(scalars, out_weight, copies):
    half = out_weight.shape[2] // 2
    return pl.pallas_call(
        panel_kernel,
        grid_spec=pltpu.PrefetchScalarGridSpec(
            num_scalar_prefetch=1,
            grid=(1,),
            in_specs=[pl.BlockSpec((1, ROWS, half), lambda i, b: (b[3], 0, b[1]))],
            out_specs=whole((copies, ROWS, half)),
        ),
        out_shape=jax.ShapeDtypeStruct((copies, ROWS, half), BF16),
        compiler_params=PARAMS,
        cost_estimate=LIGHT,
    )(scalars, out_weight)


def source(scalar_ref, k):
    return lax.rem(scalar_ref[2] - k + NY, NY)


def d_attention_kernel(scalar_ref, *refs):
    ups, mine_ref, mate_ref, out_ref, weight_ref = refs[:NY], *refs[NY:]
    half = mine_ref.shape[1]
    for side, ref in enumerate((mine_ref, mate_ref)):
        co = scalar_ref[1] if side == 0 else 1 - scalar_ref[1]
        weight_ref[:, pl.ds(pl.multiple_of(co * half, 128), half)] = ref[...]
    for k, up in enumerate(ups):
        out = lax.dot_general(weight_ref[...], up[...], NT, preferred_element_type=F32)
        out_ref[source(scalar_ref, k)] = jnp.concatenate(
            [out.astype(BF16), jnp.zeros((out.shape[0], PAD - TILE), BF16)], axis=1
        )


def d_attention(scalars, ups, w_mine, w_mate):
    dout = ups[0].shape[1]
    rows = w_mine.shape[0]
    return pl.pallas_call(
        d_attention_kernel,
        grid_spec=pltpu.PrefetchScalarGridSpec(
            num_scalar_prefetch=1,
            grid=(1,),
            in_specs=[whole((TILE, dout))] * NY + [whole(w_mine.shape)] * 2,
            out_specs=[whole((NY, rows, PAD)), whole((rows, dout))],
        ),
        out_shape=[
            jax.ShapeDtypeStruct((NY, rows, PAD), BF16),
            jax.ShapeDtypeStruct((rows, dout), BF16),
        ],
        compiler_params=PARAMS,
        cost_estimate=LIGHT,
    )(scalars, *ups, w_mine, w_mate)


def gradient_kernel(scalar_ref, att_ref, *refs):
    ups, outs = refs[: 2 * NY], refs[2 * NY :]
    att = jnp.concatenate([att_ref[source(scalar_ref, k)] for k in range(NY)], axis=1)
    rest = jnp.zeros((PAD - TILE, outs[0].shape[1]), BF16)
    for side, out_ref in enumerate(outs):
        up = jnp.concatenate(
            [block for k in range(NY) for block in (ups[side * NY + k][...], rest)], axis=0
        )
        out_ref[...] = jnp.dot(att, up, preferred_element_type=F32).astype(BF16)


def weight_gradient(scalars, atts, ups):
    half = ups[0].shape[1] // 2
    rows = atts.shape[1]
    step = 256
    steps = half // step
    mine = pl.BlockSpec((TILE, step), lambda i, b: (0, b[1] * steps + i))
    mate = pl.BlockSpec((TILE, step), lambda i, b: (0, (1 - b[1]) * steps + i))
    return pl.pallas_call(
        gradient_kernel,
        grid_spec=pltpu.PrefetchScalarGridSpec(
            num_scalar_prefetch=1,
            grid=(steps,),
            in_specs=[whole(atts.shape)] + [mine] * NY + [mate] * NY,
            out_specs=[pl.BlockSpec((rows, step), lambda i, b: (0, i))] * 2,
        ),
        out_shape=[jax.ShapeDtypeStruct((rows, half), BF16)] * 2,
        compiler_params=PARAMS,
        cost_estimate=LIGHT,
    )(scalars, atts, *ups, *ups)


def mixed_kernel(scalar_ref, att_ref, weight_ref, *outs):
    for k, out_ref in enumerate(outs):
        att = att_ref[source(scalar_ref, k)][:, :TILE]
        out = lax.dot_general(att, weight_ref[...], TN, preferred_element_type=F32)
        out_ref[...] = out.astype(BF16)


def mixed_parts(scalars, atts, weight):
    rows, dout = weight.shape
    step = 512
    return pl.pallas_call(
        mixed_kernel,
        grid_spec=pltpu.PrefetchScalarGridSpec(
            num_scalar_prefetch=1,
            grid=(dout // step,),
            in_specs=[whole(atts.shape), pl.BlockSpec((rows, step), lambda i, b: (0, i))],
            out_specs=[pl.BlockSpec((TILE, step), lambda i, b: (0, i))] * NY,
        ),
        out_shape=[jax.ShapeDtypeStruct((TILE, dout), BF16)] * NY,
        compiler_params=PARAMS,
        cost_estimate=LIGHT,
    )(scalars, atts, weight)


SWAP = [(0, 1), (1, 0)]
CROSS = [(1, 2), (2, 1)]


def shifted(x, axis, by):
    count = lax.axis_size(axis)
    return lax.ppermute(x, axis, [(i, (i + by) % count) for i in range(count)])


def swapped(x, axis):
    return lax.all_to_all(x, axis, split_axis=0, concat_axis=0, tiled=True)


def per_device(queries, keys_values, upstream, out_weight, block_pick):
    width = queries.shape[4]
    dout = upstream.shape[4]
    half = dout // 2
    rows = out_weight.shape[1]
    ny = lax.axis_size("y")
    nz = lax.axis_size("z")
    co = lax.axis_index("co")
    first = co == 0
    q = queries.reshape(TILE, width)
    kv = keys_values.reshape(2, TILE, width)
    up = upstream.reshape(TILE, dout)

    has_cross = lax.axis_index("xh") != co
    bound = jnp.where(has_cross, SLOTS * TILE, (SLOTS - 1) * TILE)
    scalars = jnp.stack([bound, co, lax.axis_index("y"), block_pick[0]]).astype(jnp.int32)

    from_time = lax.ppermute(kv, "xl", SWAP)
    from_cross = lax.ppermute(kv, ("xh", "co"), CROSS)
    from_core = lax.ppermute(kv, "co", SWAP)

    panels = panel_copies(scalars, out_weight, nz)
    w_mine = swapped(panels, "z").reshape(nz * rows, half)
    ups = [up] + [shifted(up, "y", k) for k in (1, 2, 3)]
    w_mate = lax.ppermute(w_mine, "co", SWAP)
    d_parts, w_rows = d_attention(scalars, ups, w_mine, w_mate)
    d_turned = swapped(d_parts, "y").reshape(ny, nz, rows, PAD)

    kvs = (kv, from_time, from_core, from_cross)
    att, att_turned, probs = attention_forward(scalars, q, kvs)
    atts = swapped(att_turned.reshape(ny, nz * rows, PAD), "y")

    parts = 2
    groups = HEADS // PER_STEP // parts

    def backward(c):
        gq, own, to_time, to_core, to_cross = attention_backward(
            scalars, q, kvs, att, d_turned, probs, c * groups, groups
        )
        terms = (
            lax.ppermute(to_time, "xl", SWAP),
            lax.ppermute(to_cross, ("xh", "co"), CROSS),
            lax.ppermute(to_core, "co", SWAP),
        )
        return gq, own, terms

    gq_0, own_0, terms_0 = backward(0)
    gq_1, own_1, terms_1 = backward(1)
    atts, gq_0, gq_1 = lax.optimization_barrier((atts, gq_0, gq_1))
    grad_mine, grad_mate = weight_gradient(scalars, atts, ups)
    from_mate = lax.ppermute(grad_mate, "co", SWAP)
    atts, w_rows, grad_mine = lax.optimization_barrier((atts, w_rows, grad_mine))
    mixed = mixed_parts(scalars, atts, w_rows)
    grad = (grad_mine.astype(F32) + from_mate.astype(F32)).astype(BF16).reshape(nz, rows, half)
    grad, mixed = lax.optimization_barrier((grad, mixed))
    gq_parts = (gq_0, gq_1)
    over_z = jnp.sum(swapped(grad, "z").astype(F32), axis=0).astype(BF16)
    over_z, terms_0 = lax.optimization_barrier((over_z, terms_0))
    x_near = lax.ppermute(over_z, "xl", SWAP)
    x_far = lax.ppermute(over_z, "xh", SWAP)
    x_both = lax.ppermute(over_z, ("xl", "xh"), [(i, 3 - i) for i in range(4)])
    mine = (over_z.astype(F32) + x_near.astype(F32)) + (x_far.astype(F32) + x_both.astype(F32))
    mate = lax.ppermute(mine, "co", SWAP)
    grad_weight = jnp.concatenate(
        [jnp.where(first, mine, mate), jnp.where(first, mate, mine)], axis=1
    )

    back = [shifted(mixed[k], "y", -k).astype(F32) for k in (1, 2, 3)]
    mixed = (mixed[0].astype(F32) + sum(back)).astype(BF16)
    gkv_parts = [
        own.astype(F32) + sum(t.astype(F32) for t in terms)
        for own, terms in ((own_0, terms_0), (own_1, terms_1))
    ]
    grad_q = jnp.concatenate(gq_parts, axis=1)
    grad_kv = jnp.concatenate([p.astype(BF16) for p in gkv_parts], axis=2)
    return (
        mixed.reshape(upstream.shape),
        grad_q.reshape(queries.shape),
        grad_kv.reshape(keys_values.shape),
        grad_weight,
    )


def solution(mesh):
    fine = Mesh(mesh.devices.reshape(2, 2, 2, 8, 4), ("xl", "xh", "co", "z", "y"))
    wa = ("z", "y")
    ha = ("xh", "co")
    return jax.shard_map(
        per_device,
        mesh=fine,
        in_specs=(
            P(wa, "xl", ha, None, None),
            P(None, wa, "xl", ha, None, None),
            P(wa, "xl", ha, None, None),
            P(None, wa, None),
            P(),
        ),
        out_specs=(
            P(wa, "xl", ha, None, None),
            P(wa, "xl", ha, None, None),
            P(None, wa, "xl", ha, None, None),
            P(wa, None),
        ),
        check_vma=False,
    )
```

```python
import jax
import jax.numpy as jnp
from jax import lax
from jax.experimental import pallas as pl
from jax.experimental.pallas import tpu as pltpu
from jax.sharding import Mesh, PartitionSpec as P

HEADS = 12
HEAD_DIM = 128
SCALE = HEAD_DIM ** (-0.5)
LOG2E = 1.4426950408889634
TILE = 192
SLOTS = 4
PER_STEP = 3
GROUP = PER_STEP * HEAD_DIM
ROWS = 48
NY = 4
PAD = 256
MASKED = 512
NT = (((1,), (1,)), ((), ()))
TN = (((0,), (0,)), ((), ()))
F32 = jnp.float32
BF16 = jnp.bfloat16
LIGHT = pl.CostEstimate(flops=1000, bytes_accessed=1000, transcendentals=0)
PARAMS = pltpu.CompilerParams(vmem_limit_bytes=56 * 1024 * 1024)


def window_of(refs, which, cols):
    return jnp.concatenate([ref[which, :, cols] for ref in refs], axis=0)


def probs_of(scores, bound):
    tail = scores[:, MASKED:]
    column = lax.broadcasted_iota(jnp.int32, tail.shape, 1)
    tail = jnp.where(column + MASKED < bound, tail, -1e30)
    scores = jnp.concatenate([scores[:, :MASKED], tail], axis=1)
    top = jnp.max(scores, axis=1, keepdims=True)
    weights = jnp.exp2((scores - top) * (SCALE * LOG2E))
    return weights * (1.0 / jnp.sum(weights, axis=1, keepdims=True))


def head_cols(h):
    return slice(h * HEAD_DIM, (h + 1) * HEAD_DIM)


def forward_kernel(scalar_ref, q_ref, own_ref, time_ref, core_ref, cross_ref, out_ref, out_t_ref, probs_ref):
    kv = (own_ref, time_ref, core_ref, cross_ref)
    scores = [
        lax.dot_general(
            q_ref[:, head_cols(h)], window_of(kv, 0, head_cols(h)), NT, preferred_element_type=F32
        )
        for h in range(PER_STEP)
    ]
    outs = []
    for h in range(PER_STEP):
        probs_b = probs_of(scores[h], scalar_ref[0]).astype(BF16)
        probs_ref[h] = probs_b
        v = window_of(kv, 1, head_cols(h))
        outs.append(jnp.dot(probs_b, v, preferred_element_type=F32))
    flipped = []
    for h in range(PER_STEP):
        out_ref[:, head_cols(h)] = outs[h].astype(BF16)
        flipped.append(outs[h].T.astype(BF16))
    flipped = jnp.concatenate(flipped, axis=0)
    for b in range(GROUP // ROWS):
        block = flipped[b * ROWS : (b + 1) * ROWS]
        out_t_ref[b % NY, b // NY] = jnp.concatenate([block, jnp.zeros((ROWS, PAD - TILE), BF16)], axis=1)


def backward_kernel(
    scalar_ref, q_ref, own_ref, time_ref, core_ref, cross_ref, att_ref, d_ref, probs_ref,
    gq_ref, g_own_ref, g_time_ref, g_core_ref, g_cross_ref,
):
    kv = (own_ref, time_ref, core_ref, cross_ref)
    outs = (g_own_ref, g_time_ref, g_core_ref, g_cross_ref)
    flipped = jnp.concatenate(
        [d_ref[b % NY, b // NY] for b in range(GROUP // ROWS)], axis=0
    )
    d_all = flipped.astype(F32).T[:TILE].astype(BF16)
    ds = [d_all[:, head_cols(h)] for h in range(PER_STEP)]
    d_probs = [
        lax.dot_general(ds[h], window_of(kv, 1, head_cols(h)), NT, preferred_element_type=F32)
        for h in range(PER_STEP)
    ]
    for h in range(PER_STEP):
        value_terms = lax.dot_general(probs_ref[h], ds[h], TN, preferred_element_type=F32)
        for s, ref in enumerate(outs):
            ref[1, :, head_cols(h)] = value_terms[s * TILE : (s + 1) * TILE].astype(ref.dtype)
    for h in range(PER_STEP):
        cols = head_cols(h)
        delta = jnp.sum(ds[h].astype(F32) * att_ref[:, cols].astype(F32), axis=1, keepdims=True)
        d_scores = (probs_ref[h].astype(F32) * (d_probs[h] - delta)).astype(BF16)
        key_terms = lax.dot_general(d_scores, q_ref[:, cols], TN, preferred_element_type=F32) * SCALE
        for s, ref in enumerate(outs):
            ref[0, :, cols] = key_terms[s * TILE : (s + 1) * TILE].astype(ref.dtype)
        gq = jnp.dot(d_scores, window_of(kv, 0, cols), preferred_element_type=F32) * SCALE
        gq_ref[:, cols] = gq.astype(BF16)


def flat_spec(first):
    return pl.BlockSpec((TILE, GROUP), lambda i, b: (0, i + first))


def pair_spec(first):
    return pl.BlockSpec((2, TILE, GROUP), lambda i, b: (0, 0, i + first))


def turned_spec(first):
    return pl.BlockSpec((NY, GROUP // ROWS // NY, ROWS, PAD), lambda i, b: (0, i + first, 0, 0))


def probs_spec(first):
    return pl.BlockSpec((PER_STEP, TILE, SLOTS * TILE), lambda i, b: (i + first, 0, 0))


def whole(shape):
    return pl.BlockSpec(shape, lambda *_: (0,) * len(shape))


def attention_forward(scalars, q, kvs):
    groups = HEADS // PER_STEP
    return pl.pallas_call(
        forward_kernel,
        grid_spec=pltpu.PrefetchScalarGridSpec(
            num_scalar_prefetch=1,
            grid=(groups,),
            in_specs=[flat_spec(0)] + [pair_spec(0)] * 4,
            out_specs=[flat_spec(0), turned_spec(0), probs_spec(0)],
        ),
        out_shape=[
            jax.ShapeDtypeStruct((TILE, groups * GROUP), BF16),
            jax.ShapeDtypeStruct((NY, groups * GROUP // ROWS // NY, ROWS, PAD), BF16),
            jax.ShapeDtypeStruct((HEADS, TILE, SLOTS * TILE), BF16),
        ],
        compiler_params=PARAMS,
        cost_estimate=LIGHT,
    )(scalars, q, *kvs)


def attention_backward(scalars, q, kvs, att, d, probs, first, groups):
    width = groups * GROUP
    return pl.pallas_call(
        backward_kernel,
        grid_spec=pltpu.PrefetchScalarGridSpec(
            num_scalar_prefetch=1,
            grid=(groups,),
            in_specs=[flat_spec(first)] + [pair_spec(first)] * 4 + [flat_spec(first), turned_spec(first), probs_spec(first)],
            out_specs=[flat_spec(0)] + [pair_spec(0)] * 4,
        ),
        out_shape=[jax.ShapeDtypeStruct((TILE, width), BF16)]
        + [jax.ShapeDtypeStruct((2, TILE, width), BF16)] * 4,
        compiler_params=PARAMS,
        cost_estimate=LIGHT,
    )(scalars, q, *kvs, att, d, probs)


def panel_kernel(scalar_ref, weight_ref, out_ref):
    for k in range(out_ref.shape[0]):
        out_ref[k] = weight_ref[0]


def panel_copies(scalars, out_weight, copies):
    half = out_weight.shape[2] // 2
    return pl.pallas_call(
        panel_kernel,
        grid_spec=pltpu.PrefetchScalarGridSpec(
            num_scalar_prefetch=1,
            grid=(1,),
            in_specs=[pl.BlockSpec((1, ROWS, half), lambda i, b: (b[3], 0, b[1]))],
            out_specs=whole((copies, ROWS, half)),
        ),
        out_shape=jax.ShapeDtypeStruct((copies, ROWS, half), BF16),
        compiler_params=PARAMS,
        cost_estimate=LIGHT,
    )(scalars, out_weight)


def source(scalar_ref, k):
    return lax.rem(scalar_ref[2] - k + NY, NY)


def d_attention_kernel(scalar_ref, *refs):
    ups, mine_ref, mate_ref, out_ref, weight_ref = refs[:NY], *refs[NY:]
    half = mine_ref.shape[1]
    for side, ref in enumerate((mine_ref, mate_ref)):
        co = scalar_ref[1] if side == 0 else 1 - scalar_ref[1]
        weight_ref[:, pl.ds(pl.multiple_of(co * half, 128), half)] = ref[...]
    for k, up in enumerate(ups):
        out = lax.dot_general(weight_ref[...], up[...], NT, preferred_element_type=F32)
        out_ref[source(scalar_ref, k)] = jnp.concatenate(
            [out.astype(BF16), jnp.zeros((out.shape[0], PAD - TILE), BF16)], axis=1
        )


def d_attention(scalars, ups, w_mine, w_mate):
    dout = ups[0].shape[1]
    rows = w_mine.shape[0]
    return pl.pallas_call(
        d_attention_kernel,
        grid_spec=pltpu.PrefetchScalarGridSpec(
            num_scalar_prefetch=1,
            grid=(1,),
            in_specs=[whole((TILE, dout))] * NY + [whole(w_mine.shape)] * 2,
            out_specs=[whole((NY, rows, PAD)), whole((rows, dout))],
        ),
        out_shape=[
            jax.ShapeDtypeStruct((NY, rows, PAD), BF16),
            jax.ShapeDtypeStruct((rows, dout), BF16),
        ],
        compiler_params=PARAMS,
        cost_estimate=LIGHT,
    )(scalars, *ups, w_mine, w_mate)


def gradient_kernel(scalar_ref, att_ref, *refs):
    ups, outs = refs[: 2 * NY], refs[2 * NY :]
    att = jnp.concatenate([att_ref[source(scalar_ref, k)] for k in range(NY)], axis=1)
    rest = jnp.zeros((PAD - TILE, outs[0].shape[1]), BF16)
    for side, out_ref in enumerate(outs):
        up = jnp.concatenate(
            [block for k in range(NY) for block in (ups[side * NY + k][...], rest)], axis=0
        )
        out_ref[...] = jnp.dot(att, up, preferred_element_type=F32).astype(BF16)


def weight_gradient(scalars, atts, ups):
    half = ups[0].shape[1] // 2
    rows = atts.shape[1]
    step = 256
    steps = half // step
    mine = pl.BlockSpec((TILE, step), lambda i, b: (0, b[1] * steps + i))
    mate = pl.BlockSpec((TILE, step), lambda i, b: (0, (1 - b[1]) * steps + i))
    return pl.pallas_call(
        gradient_kernel,
        grid_spec=pltpu.PrefetchScalarGridSpec(
            num_scalar_prefetch=1,
            grid=(steps,),
            in_specs=[whole(atts.shape)] + [mine] * NY + [mate] * NY,
            out_specs=[pl.BlockSpec((rows, step), lambda i, b: (0, i))] * 2,
        ),
        out_shape=[jax.ShapeDtypeStruct((rows, half), BF16)] * 2,
        compiler_params=PARAMS,
        cost_estimate=LIGHT,
    )(scalars, atts, *ups, *ups)


def mixed_kernel(scalar_ref, att_ref, weight_ref, *outs):
    for k, out_ref in enumerate(outs):
        att = att_ref[source(scalar_ref, k)][:, :TILE]
        out = lax.dot_general(att, weight_ref[...], TN, preferred_element_type=F32)
        out_ref[...] = out.astype(BF16)


def mixed_parts(scalars, atts, weight):
    rows, dout = weight.shape
    step = 512
    return pl.pallas_call(
        mixed_kernel,
        grid_spec=pltpu.PrefetchScalarGridSpec(
            num_scalar_prefetch=1,
            grid=(dout // step,),
            in_specs=[whole(atts.shape), pl.BlockSpec((rows, step), lambda i, b: (0, i))],
            out_specs=[pl.BlockSpec((TILE, step), lambda i, b: (0, i))] * NY,
        ),
        out_shape=[jax.ShapeDtypeStruct((TILE, dout), BF16)] * NY,
        compiler_params=PARAMS,
        cost_estimate=LIGHT,
    )(scalars, atts, weight)


SWAP = [(0, 1), (1, 0)]
CROSS = [(1, 2), (2, 1)]


def shifted(x, axis, by):
    count = lax.axis_size(axis)
    return lax.ppermute(x, axis, [(i, (i + by) % count) for i in range(count)])


def swapped(x, axis):
    return lax.all_to_all(x, axis, split_axis=0, concat_axis=0, tiled=True)


def per_device(queries, keys_values, upstream, out_weight, block_pick):
    width = queries.shape[4]
    dout = upstream.shape[4]
    half = dout // 2
    rows = out_weight.shape[1]
    ny = lax.axis_size("y")
    nz = lax.axis_size("z")
    co = lax.axis_index("co")
    first = co == 0
    q = queries.reshape(TILE, width)
    kv = keys_values.reshape(2, TILE, width)
    up = upstream.reshape(TILE, dout)

    has_cross = lax.axis_index("xh") != co
    bound = jnp.where(has_cross, SLOTS * TILE, (SLOTS - 1) * TILE)
    scalars = jnp.stack([bound, co, lax.axis_index("y"), block_pick[0]]).astype(jnp.int32)

    from_time = lax.ppermute(kv, "xl", SWAP)
    from_cross = lax.ppermute(kv, ("xh", "co"), CROSS)
    from_core = lax.ppermute(kv, "co", SWAP)

    panels = panel_copies(scalars, out_weight, nz)
    w_mine = swapped(panels, "z").reshape(nz * rows, half)
    ups = [up] + [shifted(up, "y", k) for k in (1, 2, 3)]
    w_mate = lax.ppermute(w_mine, "co", SWAP)
    d_parts, w_rows = d_attention(scalars, ups, w_mine, w_mate)
    d_turned = swapped(d_parts, "y").reshape(ny, nz, rows, PAD)

    kvs = (kv, from_time, from_core, from_cross)
    att, att_turned, probs = attention_forward(scalars, q, kvs)
    atts = swapped(att_turned.reshape(ny, nz * rows, PAD), "y")

    parts = 2
    groups = HEADS // PER_STEP // parts

    def backward(c):
        gq, own, to_time, to_core, to_cross = attention_backward(
            scalars, q, kvs, att, d_turned, probs, c * groups, groups
        )
        from_time = lax.ppermute(to_time, "xl", SWAP)
        from_cross = lax.ppermute(to_cross, ("xh", "co"), CROSS)
        return gq, own, (from_time, from_cross), to_core

    gq_0, own_0, terms_0, to_core = backward(0)
    terms_0 += (lax.ppermute(to_core, "co", SWAP),)
    gq_1, own_1, terms_1, to_core = backward(1)
    atts, gq_0, gq_1 = lax.optimization_barrier((atts, gq_0, gq_1))
    grad_mine, grad_mate = weight_gradient(scalars, atts, ups)
    from_mate = lax.ppermute(grad_mate, "co", SWAP)
    atts, w_rows, grad_mine = lax.optimization_barrier((atts, w_rows, grad_mine))
    mixed = mixed_parts(scalars, atts, w_rows)
    grad = (grad_mine.astype(F32) + from_mate.astype(F32)).astype(BF16).reshape(nz, rows, half)
    grad, mixed = lax.optimization_barrier((grad, mixed))
    gq_parts = (gq_0, gq_1)
    over_z = jnp.sum(swapped(grad, "z").astype(F32), axis=0).astype(BF16)
    over_z, terms_0, to_core = lax.optimization_barrier((over_z, terms_0, to_core))
    x_near = lax.ppermute(over_z, "xl", SWAP)
    x_far = lax.ppermute(over_z, "xh", SWAP)
    x_both = lax.ppermute(over_z, ("xl", "xh"), [(i, 3 - i) for i in range(4)])
    mine = (over_z.astype(F32) + x_near.astype(F32)) + (x_far.astype(F32) + x_both.astype(F32))
    mate = lax.ppermute(mine, "co", SWAP)
    grad_weight = jnp.concatenate(
        [jnp.where(first, mine, mate), jnp.where(first, mate, mine)], axis=1
    )

    back = [shifted(mixed[k], "y", -k) for k in (1, 2, 3)]
    back, _ = lax.optimization_barrier((back, x_near))
    mixed = (mixed[0].astype(F32) + sum(b.astype(F32) for b in back)).astype(BF16)
    terms_1 += (lax.ppermute(to_core, "co", SWAP),)
    gkv_parts = [
        own.astype(F32) + sum(t.astype(F32) for t in terms)
        for own, terms in ((own_0, terms_0), (own_1, terms_1))
    ]
    grad_q = jnp.concatenate(gq_parts, axis=1)
    grad_kv = jnp.concatenate([p.astype(BF16) for p in gkv_parts], axis=2)
    return (
        mixed.reshape(upstream.shape),
        grad_q.reshape(queries.shape),
        grad_kv.reshape(keys_values.shape),
        grad_weight,
    )


def solution(mesh):
    fine = Mesh(mesh.devices.reshape(2, 2, 2, 8, 4), ("xl", "xh", "co", "z", "y"))
    wa = ("z", "y")
    ha = ("xh", "co")
    return jax.shard_map(
        per_device,
        mesh=fine,
        in_specs=(
            P(wa, "xl", ha, None, None),
            P(None, wa, "xl", ha, None, None),
            P(wa, "xl", ha, None, None),
            P(None, wa, None),
            P(),
        ),
        out_specs=(
            P(wa, "xl", ha, None, None),
            P(wa, "xl", ha, None, None),
            P(None, wa, "xl", ha, None, None),
            P(wa, None),
        ),
        check_vma=False,
    )
```

```python
import jax
import jax.numpy as jnp
from jax import lax
from jax.experimental import pallas as pl
from jax.experimental.pallas import tpu as pltpu
from jax.sharding import Mesh, PartitionSpec as P

HEADS = 12
HEAD_DIM = 128
SCALE = HEAD_DIM ** (-0.5)
LOG2E = 1.4426950408889634
TILE = 192
SLOTS = 4
PER_STEP = 3
GROUP = PER_STEP * HEAD_DIM
ROWS = 48
NY = 4
PAD = 256
MASKED = 512
NT = (((1,), (1,)), ((), ()))
TN = (((0,), (0,)), ((), ()))
F32 = jnp.float32
BF16 = jnp.bfloat16
LIGHT = pl.CostEstimate(flops=1000, bytes_accessed=1000, transcendentals=0)
PARAMS = pltpu.CompilerParams(vmem_limit_bytes=56 * 1024 * 1024)


def window_of(refs, which, cols):
    return jnp.concatenate([ref[which, :, cols] for ref in refs], axis=0)


def probs_of(scores, bound):
    tail = scores[:, MASKED:]
    column = lax.broadcasted_iota(jnp.int32, tail.shape, 1)
    tail = jnp.where(column + MASKED < bound, tail, -1e30)
    scores = jnp.concatenate([scores[:, :MASKED], tail], axis=1)
    top = jnp.max(scores, axis=1, keepdims=True)
    weights = jnp.exp2((scores - top) * (SCALE * LOG2E))
    return weights * (1.0 / jnp.sum(weights, axis=1, keepdims=True))


def head_cols(h):
    return slice(h * HEAD_DIM, (h + 1) * HEAD_DIM)


def forward_kernel(scalar_ref, q_ref, own_ref, time_ref, core_ref, cross_ref, out_ref, out_t_ref, probs_ref):
    kv = (own_ref, time_ref, core_ref, cross_ref)
    scores = [
        lax.dot_general(
            q_ref[:, head_cols(h)], window_of(kv, 0, head_cols(h)), NT, preferred_element_type=F32
        )
        for h in range(PER_STEP)
    ]
    outs = []
    for h in range(PER_STEP):
        probs_b = probs_of(scores[h], scalar_ref[0]).astype(BF16)
        probs_ref[h] = probs_b
        v = window_of(kv, 1, head_cols(h))
        outs.append(jnp.dot(probs_b, v, preferred_element_type=F32))
    flipped = []
    for h in range(PER_STEP):
        out_ref[:, head_cols(h)] = outs[h].astype(BF16)
        flipped.append(outs[h].T.astype(BF16))
    flipped = jnp.concatenate(flipped, axis=0)
    for b in range(GROUP // ROWS):
        block = flipped[b * ROWS : (b + 1) * ROWS]
        out_t_ref[b % NY, b // NY] = jnp.concatenate([block, jnp.zeros((ROWS, PAD - TILE), BF16)], axis=1)


def backward_kernel(
    scalar_ref, q_ref, own_ref, time_ref, core_ref, cross_ref, att_ref, d_ref, probs_ref,
    gq_ref, g_own_ref, g_time_ref, g_core_ref, g_cross_ref,
):
    kv = (own_ref, time_ref, core_ref, cross_ref)
    outs = (g_own_ref, g_time_ref, g_core_ref, g_cross_ref)
    flipped = jnp.concatenate(
        [d_ref[b % NY, b // NY] for b in range(GROUP // ROWS)], axis=0
    )
    d_all = flipped.astype(F32).T[:TILE].astype(BF16)
    ds = [d_all[:, head_cols(h)] for h in range(PER_STEP)]
    d_probs = [
        lax.dot_general(ds[h], window_of(kv, 1, head_cols(h)), NT, preferred_element_type=F32)
        for h in range(PER_STEP)
    ]
    for h in range(PER_STEP):
        value_terms = lax.dot_general(probs_ref[h], ds[h], TN, preferred_element_type=F32)
        for s, ref in enumerate(outs):
            ref[1, :, head_cols(h)] = value_terms[s * TILE : (s + 1) * TILE].astype(ref.dtype)
    for h in range(PER_STEP):
        cols = head_cols(h)
        delta = jnp.sum(ds[h].astype(F32) * att_ref[:, cols].astype(F32), axis=1, keepdims=True)
        d_scores = (probs_ref[h].astype(F32) * (d_probs[h] - delta)).astype(BF16)
        key_terms = lax.dot_general(d_scores, q_ref[:, cols], TN, preferred_element_type=F32) * SCALE
        for s, ref in enumerate(outs):
            ref[0, :, cols] = key_terms[s * TILE : (s + 1) * TILE].astype(ref.dtype)
        gq = jnp.dot(d_scores, window_of(kv, 0, cols), preferred_element_type=F32) * SCALE
        gq_ref[:, cols] = gq.astype(BF16)


def flat_spec(first):
    return pl.BlockSpec((TILE, GROUP), lambda i, b: (0, i + first))


def pair_spec(first):
    return pl.BlockSpec((2, TILE, GROUP), lambda i, b: (0, 0, i + first))


def turned_spec(first):
    return pl.BlockSpec((NY, GROUP // ROWS // NY, ROWS, PAD), lambda i, b: (0, i + first, 0, 0))


def probs_spec(first):
    return pl.BlockSpec((PER_STEP, TILE, SLOTS * TILE), lambda i, b: (i + first, 0, 0))


def whole(shape):
    return pl.BlockSpec(shape, lambda *_: (0,) * len(shape))


def attention_forward(scalars, q, kvs):
    groups = HEADS // PER_STEP
    return pl.pallas_call(
        forward_kernel,
        grid_spec=pltpu.PrefetchScalarGridSpec(
            num_scalar_prefetch=1,
            grid=(groups,),
            in_specs=[flat_spec(0)] + [pair_spec(0)] * 4,
            out_specs=[flat_spec(0), turned_spec(0), probs_spec(0)],
        ),
        out_shape=[
            jax.ShapeDtypeStruct((TILE, groups * GROUP), BF16),
            jax.ShapeDtypeStruct((NY, groups * GROUP // ROWS // NY, ROWS, PAD), BF16),
            jax.ShapeDtypeStruct((HEADS, TILE, SLOTS * TILE), BF16),
        ],
        compiler_params=PARAMS,
        cost_estimate=LIGHT,
    )(scalars, q, *kvs)


def attention_backward(scalars, q, kvs, att, d, probs, first, groups):
    width = groups * GROUP
    return pl.pallas_call(
        backward_kernel,
        grid_spec=pltpu.PrefetchScalarGridSpec(
            num_scalar_prefetch=1,
            grid=(groups,),
            in_specs=[flat_spec(first)] + [pair_spec(first)] * 4 + [flat_spec(first), turned_spec(first), probs_spec(first)],
            out_specs=[flat_spec(0)] + [pair_spec(0)] * 4,
        ),
        out_shape=[jax.ShapeDtypeStruct((TILE, width), BF16)]
        + [jax.ShapeDtypeStruct((2, TILE, width), BF16)] * 4,
        compiler_params=PARAMS,
        cost_estimate=LIGHT,
    )(scalars, q, *kvs, att, d, probs)


def panel_kernel(scalar_ref, weight_ref, out_ref):
    for k in range(out_ref.shape[0]):
        out_ref[k] = weight_ref[0]


def panel_copies(scalars, out_weight, copies):
    half = out_weight.shape[2] // 2
    return pl.pallas_call(
        panel_kernel,
        grid_spec=pltpu.PrefetchScalarGridSpec(
            num_scalar_prefetch=1,
            grid=(1,),
            in_specs=[pl.BlockSpec((1, ROWS, half), lambda i, b: (b[3], 0, b[1]))],
            out_specs=whole((copies, ROWS, half)),
        ),
        out_shape=jax.ShapeDtypeStruct((copies, ROWS, half), BF16),
        compiler_params=PARAMS,
        cost_estimate=LIGHT,
    )(scalars, out_weight)


def source(scalar_ref, k):
    return lax.rem(scalar_ref[2] - k + NY, NY)


def d_attention_kernel(scalar_ref, *refs):
    ups, mine_ref, mate_ref, out_ref, weight_ref = refs[:NY], *refs[NY:]
    half = mine_ref.shape[1]
    for side, ref in enumerate((mine_ref, mate_ref)):
        co = scalar_ref[1] if side == 0 else 1 - scalar_ref[1]
        weight_ref[:, pl.ds(pl.multiple_of(co * half, 128), half)] = ref[...]
    for k, up in enumerate(ups):
        out = lax.dot_general(weight_ref[...], up[...], NT, preferred_element_type=F32)
        out_ref[source(scalar_ref, k)] = jnp.concatenate(
            [out.astype(BF16), jnp.zeros((out.shape[0], PAD - TILE), BF16)], axis=1
        )


def d_attention(scalars, ups, w_mine, w_mate):
    dout = ups[0].shape[1]
    rows = w_mine.shape[0]
    return pl.pallas_call(
        d_attention_kernel,
        grid_spec=pltpu.PrefetchScalarGridSpec(
            num_scalar_prefetch=1,
            grid=(1,),
            in_specs=[whole((TILE, dout))] * NY + [whole(w_mine.shape)] * 2,
            out_specs=[whole((NY, rows, PAD)), whole((rows, dout))],
        ),
        out_shape=[
            jax.ShapeDtypeStruct((NY, rows, PAD), BF16),
            jax.ShapeDtypeStruct((rows, dout), BF16),
        ],
        compiler_params=PARAMS,
        cost_estimate=LIGHT,
    )(scalars, *ups, w_mine, w_mate)


def gradient_kernel(scalar_ref, att_ref, *refs):
    ups, outs = refs[: 2 * NY], refs[2 * NY :]
    att = jnp.concatenate([att_ref[source(scalar_ref, k)] for k in range(NY)], axis=1)
    rest = jnp.zeros((PAD - TILE, outs[0].shape[1]), BF16)
    for side, out_ref in enumerate(outs):
        up = jnp.concatenate(
            [block for k in range(NY) for block in (ups[side * NY + k][...], rest)], axis=0
        )
        out_ref[...] = jnp.dot(att, up, preferred_element_type=F32).astype(BF16)


def weight_gradient(scalars, atts, ups):
    half = ups[0].shape[1] // 2
    rows = atts.shape[1]
    step = 256
    steps = half // step
    mine = pl.BlockSpec((TILE, step), lambda i, b: (0, b[1] * steps + i))
    mate = pl.BlockSpec((TILE, step), lambda i, b: (0, (1 - b[1]) * steps + i))
    return pl.pallas_call(
        gradient_kernel,
        grid_spec=pltpu.PrefetchScalarGridSpec(
            num_scalar_prefetch=1,
            grid=(steps,),
            in_specs=[whole(atts.shape)] + [mine] * NY + [mate] * NY,
            out_specs=[pl.BlockSpec((rows, step), lambda i, b: (0, i))] * 2,
        ),
        out_shape=[jax.ShapeDtypeStruct((rows, half), BF16)] * 2,
        compiler_params=PARAMS,
        cost_estimate=LIGHT,
    )(scalars, atts, *ups, *ups)


def mixed_kernel(scalar_ref, att_ref, weight_ref, *outs):
    for k, out_ref in enumerate(outs):
        att = att_ref[source(scalar_ref, k)][:, :TILE]
        out = lax.dot_general(att, weight_ref[...], TN, preferred_element_type=F32)
        out_ref[...] = out.astype(BF16)


def mixed_parts(scalars, atts, weight):
    rows, dout = weight.shape
    step = 512
    return pl.pallas_call(
        mixed_kernel,
        grid_spec=pltpu.PrefetchScalarGridSpec(
            num_scalar_prefetch=1,
            grid=(dout // step,),
            in_specs=[whole(atts.shape), pl.BlockSpec((rows, step), lambda i, b: (0, i))],
            out_specs=[pl.BlockSpec((TILE, step), lambda i, b: (0, i))] * NY,
        ),
        out_shape=[jax.ShapeDtypeStruct((TILE, dout), BF16)] * NY,
        compiler_params=PARAMS,
        cost_estimate=LIGHT,
    )(scalars, atts, weight)


SWAP = [(0, 1), (1, 0)]
CROSS = [(1, 2), (2, 1)]


def shifted(x, axis, by):
    count = lax.axis_size(axis)
    return lax.ppermute(x, axis, [(i, (i + by) % count) for i in range(count)])


def swapped(x, axis):
    return lax.all_to_all(x, axis, split_axis=0, concat_axis=0, tiled=True)


def per_device(queries, keys_values, upstream, out_weight, block_pick):
    width = queries.shape[4]
    dout = upstream.shape[4]
    half = dout // 2
    rows = out_weight.shape[1]
    ny = lax.axis_size("y")
    nz = lax.axis_size("z")
    co = lax.axis_index("co")
    first = co == 0
    q = queries.reshape(TILE, width)
    kv = keys_values.reshape(2, TILE, width)
    up = upstream.reshape(TILE, dout)

    has_cross = lax.axis_index("xh") != co
    bound = jnp.where(has_cross, SLOTS * TILE, (SLOTS - 1) * TILE)
    scalars = jnp.stack([bound, co, lax.axis_index("y"), block_pick[0]]).astype(jnp.int32)

    from_time = lax.ppermute(kv, "xl", SWAP)
    from_cross = lax.ppermute(kv, ("xh", "co"), CROSS)
    from_core = lax.ppermute(kv, "co", SWAP)

    panels = panel_copies(scalars, out_weight, nz)
    w_mine = swapped(panels, "z").reshape(nz * rows, half)
    ups = [up] + [shifted(up, "y", k) for k in (1, 2, 3)]
    w_mate = lax.ppermute(w_mine, "co", SWAP)
    d_parts, w_rows = d_attention(scalars, ups, w_mine, w_mate)
    d_turned = swapped(d_parts, "y").reshape(ny, nz, rows, PAD)

    kvs = (kv, from_time, from_core, from_cross)
    att, att_turned, probs = attention_forward(scalars, q, kvs)
    atts = swapped(att_turned.reshape(ny, nz * rows, PAD), "y")

    parts = 2
    groups = HEADS // PER_STEP // parts

    def backward(c):
        gq, own, to_time, to_core, to_cross = attention_backward(
            scalars, q, kvs, att, d_turned, probs, c * groups, groups
        )
        terms = (
            lax.ppermute(to_time, "xl", SWAP),
            lax.ppermute(to_cross, ("xh", "co"), CROSS),
            lax.ppermute(to_core, "co", SWAP),
        )
        return gq, own, terms

    gq_0, own_0, terms_0 = backward(0)
    atts, gq_0 = lax.optimization_barrier((atts, gq_0))
    grad_mine, grad_mate = weight_gradient(scalars, atts, ups)
    from_mate = lax.ppermute(grad_mate, "co", SWAP)
    atts, w_rows, grad_mine = lax.optimization_barrier((atts, w_rows, grad_mine))
    mixed = mixed_parts(scalars, atts, w_rows)
    grad = (grad_mine.astype(F32) + from_mate.astype(F32)).astype(BF16).reshape(nz, rows, half)
    probs, grad, mixed = lax.optimization_barrier((probs, grad, mixed))
    gq_1, own_1, terms_1 = backward(1)
    gkv_parts = [
        own.astype(F32) + sum(t.astype(F32) for t in terms)
        for own, terms in ((own_0, terms_0), (own_1, terms_1))
    ]
    gq_parts = (gq_0, gq_1)
    over_z = jnp.sum(swapped(grad, "z").astype(F32), axis=0).astype(BF16)
    x_near = lax.ppermute(over_z, "xl", SWAP)
    x_far = lax.ppermute(over_z, "xh", SWAP)
    x_both = lax.ppermute(over_z, ("xl", "xh"), [(i, 3 - i) for i in range(4)])
    mine = (over_z.astype(F32) + x_near.astype(F32)) + (x_far.astype(F32) + x_both.astype(F32))
    mate = lax.ppermute(mine, "co", SWAP)
    grad_weight = jnp.concatenate(
        [jnp.where(first, mine, mate), jnp.where(first, mate, mine)], axis=1
    )

    back = [shifted(mixed[k], "y", -k) for k in (1, 2, 3)]
    back, _ = lax.optimization_barrier((back, x_near))
    mixed = (mixed[0].astype(F32) + sum(b.astype(F32) for b in back)).astype(BF16)
    grad_q = jnp.concatenate(gq_parts, axis=1)
    grad_kv = jnp.concatenate([p.astype(BF16) for p in gkv_parts], axis=2)
    return (
        mixed.reshape(upstream.shape),
        grad_q.reshape(queries.shape),
        grad_kv.reshape(keys_values.shape),
        grad_weight,
    )


def solution(mesh):
    fine = Mesh(mesh.devices.reshape(2, 2, 2, 8, 4), ("xl", "xh", "co", "z", "y"))
    wa = ("z", "y")
    ha = ("xh", "co")
    return jax.shard_map(
        per_device,
        mesh=fine,
        in_specs=(
            P(wa, "xl", ha, None, None),
            P(None, wa, "xl", ha, None, None),
            P(wa, "xl", ha, None, None),
            P(None, wa, None),
            P(),
        ),
        out_specs=(
            P(wa, "xl", ha, None, None),
            P(wa, "xl", ha, None, None),
            P(None, wa, "xl", ha, None, None),
            P(wa, None),
        ),
        check_vma=False,
    )
```
